256 devices in a mesh: ctx: 16 (over x_lo, z), exp: 16 (over x_hi, y, core).
Axes of the slice: x: 4 (x_hi: 2, x_lo: 2; x = x_hi * 2 + x_lo), y: 4, z: 8, core: 2. Of those that a mesh axis runs over, the one named last changes fastest.
Arguments:
- tokens: bfloat16 [16384, 2048], P(('ctx', 'exp')), may hold values from -6 to 6
- attn_gain: float32 [2048], replicated, may hold values from 0.1 to 1.9
- query_gain: float32 [128], replicated, may hold values from 1 to 2.4
- key_gain: float32 [128], replicated, may hold values from 1 to 2.4
- query_weight: bfloat16 [2048, 2048], P(None, 'exp'), may hold values from -0.125 to 0.125
- key_weight: bfloat16 [2048, 256], replicated, may hold values from -0.125 to 0.125
- value_weight: bfloat16 [2048, 256], replicated, may hold values from -0.125 to 0.125
- out_weight: bfloat16 [2048, 2048], P('exp'), may hold values from -0.125 to 0.125
- moe_gain: float32 [2048], replicated, may hold values from 0.1 to 1.9
- route_ids: int32 [16384, 8], P(('ctx', 'exp')), may hold values from 0 to 15, all different within a row; in each aligned block of 64 rows (0 to 63, 64 to 127, ...) at most 48 rows name the same one
- route_weights: float32 [16384, 8], P(('ctx', 'exp')), may hold values from 0.02 to 0.4
- gate_weight: bfloat16 [16, 2048, 768], P('exp'), may hold values from -0.125 to 0.125
- up_weight: bfloat16 [16, 2048, 768], P('exp'), may hold values from -0.125 to 0.125
- down_weight: bfloat16 [16, 768, 2048], P('exp'), may hold values from -0.21875 to 0.21875
Outputs:
- layer_out: bfloat16 [16384, 2048], P(('ctx', 'exp'))
The draws below stay inside these ranges and needn't reach their ends.
Inputs may be any that keep to these rules, and one draw needn't show every extreme that they name: `route_ids`: each row names 8 different experts; within the rows of one device no expert is named by more than 48 rows.
All inputs are finite; a program needn't handle non-finite values.
Results may differ from the reference program's by a relative error of at most 0.017.
Values may be sent and summed in bfloat16 or wider, within the bound.
No kernel may reach another device: no remote copies, remote signals or barrier semaphores. Data moves between devices by JAX's collectives and lax.ppermute only.
A program may use at most 128 MiB of HBM per device.

```python
import math
import jax
import jax.numpy as jnp
import numpy as np
from jax import lax

D = 2048
HEADS = 16
KVH = 2
HD = 128
FF = 768
TOPK = 8
SEQ_DEV = 1024
SEQ = 16384
TOK_MOE = 64
EXPERTS_LIVE = 16
CAP = 48
N_CTX = 16


def levels(stream_key, shape, cuts, low, top_value):
    factor_of, own = 1.0, jax.random.fold_in(stream_key, 6)
    for axis_at, parts in cuts:
        draws = jnp.exp(jax.random.uniform(jax.random.fold_in(own, axis_at), (parts,), jnp.float32, low / len(cuts), top_value / len(cuts)))
        factor_of = factor_of * jnp.repeat(draws, shape[axis_at] // parts).reshape([-1 if axis == axis_at else 1 for axis in range(len(shape))])
    return factor_of


def assign_block(stream_key, own, number, rows, count, top, limit, slope):
    order = jax.random.permutation(stream_key, count)
    heavy_load, ordinary = load_shares(count, rows * top, limit, slope, True), load_shares(count, rows * top, limit, slope, False)
    places = jnp.arange(count)

    def named(tallies, turn):
        used = int((tallies > 0).sum())
        fixed = max(1, used // 4)
        shifted = fixed + (places - fixed + turn * (used - fixed)) % max(1, count - fixed)
        return jnp.zeros((count,), jnp.int32).at[order[jnp.where(places < fixed, places, shifted)]].set(jnp.asarray(tallies, jnp.int32))

    tallies = jnp.where(number % 4 == 0, named(heavy_load, number // 4), named(ordinary, number - number // 4 - 1))
    mixed = jax.random.permutation(jax.random.fold_in(own, 3), count)
    giver, receiver = mixed[0:count // 2 * 2:2], mixed[1:count // 2 * 2:2]
    margin = jnp.minimum(tallies[giver] - 1, limit - tallies[receiver]) // 2
    margin = jnp.where((giver == order[0]) | (receiver == order[0]) | (tallies[receiver] == 0), 0, jnp.maximum(margin, 0))
    shifted = jax.random.randint(jax.random.fold_in(own, 4), (count // 2,), 0, 1 << 20) % (margin + 1)
    tallies = tallies.at[giver].add(-shifted).at[receiver].add(shifted)
    labels = jnp.searchsorted(jnp.cumsum(tallies), jnp.arange(rows * top), side="right").astype(jnp.int32)
    listing = labels.reshape(top, rows).T
    listing = listing[jax.random.permutation(jax.random.fold_in(own, 1), rows)]
    turn = jax.random.randint(jax.random.fold_in(own, 2), (rows, 1), 0, top)
    return jnp.take_along_axis(listing, (jnp.arange(top)[None, :] + turn) % top, axis=1)


def load_shares(number_of, total, limit, slope, full):
    loads = [(1 << 20) // math.isqrt(rank ** slope) + 1 for rank in range(1, number_of + 1)]
    largest = limit if full else min(limit, max(-(-total // number_of), total * loads[0] // sum(loads)))
    least = 1 if total - largest >= number_of - 1 else 0
    given, rest = [largest] + [least] * (number_of - 1), total - largest - least * (number_of - 1)
    while rest > 0:
        free = [i for i in range(1, number_of) if given[i] < largest] or [i for i in range(1, number_of) if given[i] < limit]
        mass, remaining = sum([loads[i] for i in free]), rest
        for i in free:
            addition = min(limit - given[i], max(1, remaining * loads[i] // mass), rest)
            given[i] = given[i] + addition
            rest = rest - addition
    return np.array(given)


def normal_values(rng, extent, scale, bound, shards=(), kind=jnp.bfloat16):
    loudness = levels(rng, extent, shards, -0.22, 0.18) if shards else 1.0
    values = jax.random.normal(rng, extent, jnp.float32) * scale * loudness
    return jnp.minimum(jnp.maximum(values, -bound), bound).astype(kind)


def setup_inputs(seed: int = 0) -> dict:
    key_list = jax.random.split(jax.random.key(seed), 15)
    tokens = normal_values(key_list[0], (SEQ, D), 1.0, 6.0, ((0, 256),))
    attn_gain = jnp.clip(1.0 + 0.18 * jax.random.normal(key_list[1], (D,), jnp.float32), 0.1, 1.9)
    query_gain = jnp.clip(jnp.exp(jax.random.uniform(key_list[2], (HD,), jnp.float32, math.log(1.0), math.log(2.4))), 1.0, 2.4)
    key_gain = jnp.clip(jnp.exp(jax.random.uniform(key_list[3], (HD,), jnp.float32, math.log(1.0), math.log(2.4))), 1.0, 2.4)
    query_weight = normal_values(key_list[4], (D, HEADS * HD), D ** -0.5, 0.125, ((1, 16),))
    key_weight = normal_values(key_list[5], (D, KVH * HD), D ** -0.5, 0.125)
    value_weight = normal_values(key_list[6], (D, KVH * HD), D ** -0.5, 0.125)
    out_weight = normal_values(key_list[7], (HEADS * HD, D), (HEADS * HD) ** -0.5, 0.125, ((0, 16),))
    moe_gain = jnp.clip(1.0 + 0.18 * jax.random.normal(key_list[8], (D,), jnp.float32), 0.1, 1.9)
    route_ids_keys = jax.random.split(jax.random.fold_in(key_list[9], 1), SEQ // TOK_MOE)
    route_ids_turns = jax.random.permutation(jax.random.fold_in(key_list[9], 3), SEQ // TOK_MOE)
    route_ids = jax.vmap(lambda own, number: assign_block(jax.random.fold_in(key_list[9], 2), own, number, TOK_MOE, EXPERTS_LIVE, TOPK, CAP, 2))(route_ids_keys, route_ids_turns).reshape((SEQ, TOPK))
    route_weights = jnp.clip(jnp.exp(math.log(0.4) - 2.9957323 * jax.random.uniform(key_list[10], (SEQ, TOPK), jnp.float32) ** levels(key_list[10], (SEQ, TOPK), ((0, 256),), -0.2, 0.2)), 0.02, 0.4)
    gate_weight = normal_values(key_list[11], (EXPERTS_LIVE, D, FF), D ** -0.5, 0.125, ((0, 16),))
    up_weight = normal_values(key_list[12], (EXPERTS_LIVE, D, FF), D ** -0.5, 0.125, ((0, 16),))
    down_weight = normal_values(key_list[13], (EXPERTS_LIVE, FF, D), FF ** -0.5, 0.21875, ((0, 16),))
    return {"tokens": tokens, "attn_gain": attn_gain, "query_gain": query_gain, "key_gain": key_gain, "query_weight": query_weight, "key_weight": key_weight, "value_weight": value_weight, "out_weight": out_weight, "moe_gain": moe_gain, "route_ids": route_ids, "route_weights": route_weights, "gate_weight": gate_weight, "up_weight": up_weight, "down_weight": down_weight}


epsilon = 1e-06
rope_base = 1000000.0

def rms_norm(values, gain):
    values = values.astype(jnp.float32)
    factor = lax.rsqrt(lax.optimization_barrier(jnp.mean(values * values, axis=-1, keepdims=True)) + epsilon)
    return values * factor * gain

def rotary(values, positions):
    half_dim = values.shape[-1] // 2
    exponent = jnp.arange(half_dim, dtype=jnp.float32) * (2.0 / values.shape[-1])
    inverse = jnp.power(jnp.float32(rope_base), -exponent)
    angles = positions[:, None] * inverse[None, :]
    cosine = jnp.cos(angles)[:, None, :]
    sine = jnp.sin(angles)[:, None, :]
    first_half = values[..., :half_dim]
    second_half = values[..., half_dim:]
    return jnp.concatenate([first_half * cosine - second_half * sine, second_half * cosine + first_half * sine], axis=-1)

def reference(tokens, attn_gain, query_gain, key_gain, query_weight, key_weight, value_weight, out_weight, moe_gain, route_ids, route_weights, gate_weight, up_weight, down_weight):
    normed = rms_norm(tokens, attn_gain).astype(jnp.bfloat16)
    positions = jnp.arange(SEQ, dtype=jnp.int32).astype(jnp.float32)
    queries = jnp.dot(normed, query_weight, preferred_element_type=jnp.float32).reshape(SEQ, HEADS, HD)
    queries = rotary(rms_norm(queries, query_gain), positions).astype(jnp.bfloat16)
    keys_all = jnp.dot(normed, key_weight, preferred_element_type=jnp.float32).reshape(SEQ, KVH, HD)
    keys_all = rotary(rms_norm(keys_all, key_gain), positions).astype(jnp.bfloat16)
    values_all = jnp.dot(normed, value_weight, preferred_element_type=jnp.float32).astype(jnp.bfloat16).reshape(SEQ, KVH, HD)
    score_scale = HD ** (-0.5)
    group_size = HEADS // KVH
    key_index = jnp.arange(SEQ, dtype=jnp.int32)

    def one_head(head_index):
        query_head = lax.dynamic_index_in_dim(queries, head_index, 1, keepdims=False)
        shared = (head_index // group_size).astype(jnp.int32)
        key_head = lax.dynamic_index_in_dim(keys_all, shared, 1, keepdims=False)
        value_head = lax.dynamic_index_in_dim(values_all, shared, 1, keepdims=False)

        def one_block(block_start):
            query_rows = lax.dynamic_slice_in_dim(query_head, block_start, SEQ_DEV, 0)
            scores = lax.dot_general(query_rows, key_head, (((1,), (1,)), ((), ())), preferred_element_type=jnp.float32) * score_scale
            query_index = block_start + jnp.arange(SEQ_DEV, dtype=jnp.int32)
            allowed = key_index[None, :] <= query_index[:, None]
            weights = jnp.where(allowed, jnp.exp(scores), 0.0)
            numerator = jnp.dot(weights.astype(jnp.bfloat16), value_head, preferred_element_type=jnp.float32)
            denominator = lax.optimization_barrier(jnp.sum(weights, axis=1))
            return (numerator / denominator[:, None]).astype(jnp.bfloat16)
        starts = jnp.arange(N_CTX, dtype=jnp.int32) * SEQ_DEV
        return lax.map(one_block, starts).reshape(SEQ, HD)
    attended = lax.map(one_head, jnp.arange(HEADS, dtype=jnp.int32))
    attended = jnp.transpose(attended, (1, 0, 2)).reshape(SEQ, HEADS * HD)
    projected = jnp.dot(attended, out_weight, preferred_element_type=jnp.float32)
    hidden = (tokens.astype(jnp.float32) + projected).astype(jnp.bfloat16)
    moe_input = rms_norm(hidden, moe_gain).astype(jnp.bfloat16)

    def one_expert(totals, expert):
        gate_proj = jnp.dot(moe_input, gate_weight[expert], preferred_element_type=jnp.float32)
        up_proj = jnp.dot(moe_input, up_weight[expert], preferred_element_type=jnp.float32)
        inner_act = (jax.nn.silu(gate_proj) * up_proj).astype(jnp.bfloat16)
        result = jnp.dot(inner_act, down_weight[expert], preferred_element_type=jnp.float32).astype(jnp.bfloat16)
        factor = lax.optimization_barrier(jnp.sum(jnp.where(route_ids == expert, route_weights, 0.0), axis=1))
        return (totals + factor[:, None] * result.astype(jnp.float32), None)
    mixture, unused = lax.scan(one_expert, jnp.zeros((SEQ, D), jnp.float32), jnp.arange(EXPERTS_LIVE, dtype=jnp.int32))
    return (hidden.astype(jnp.float32) + mixture).astype(jnp.bfloat16)
```

```python
import functools

import jax
import jax.numpy as jnp
from jax import lax
from jax.experimental import pallas as pl
from jax.experimental.pallas import tpu as pltpu
from jax.sharding import PartitionSpec as P

EPS = 1e-06
ROPE_BASE = 1000000.0
HD = 128
D = 2048
FF = 768
ROWS = 64
WIDE = 8 * HD + 128
LOG2E = 1.4426950408889634
MB = 1 << 20
BF = jnp.bfloat16
F32 = jnp.float32

VM = pl.BlockSpec(memory_space=pltpu.VMEM)
SM = pl.BlockSpec(memory_space=pltpu.SMEM)


def call(kernel, args, outs, flops=0, moved=0, scratch=(), scalars=True, limit=40):
    specs = [SM] + [VM] * (len(args) - 1) if scalars else [VM] * len(args)
    return pl.pallas_call(
        kernel,
        out_shape=[jax.ShapeDtypeStruct(s, t) for s, t in outs],
        in_specs=specs,
        out_specs=[VM] * len(outs),
        scratch_shapes=list(scratch),
        compiler_params=pltpu.CompilerParams(vmem_limit_bytes=limit * MB),
        cost_estimate=pl.CostEstimate(flops=flops, bytes_accessed=moved, transcendentals=0),
    )(*args)


def rms(values, gain):
    factor = lax.rsqrt(jnp.mean(values * values, axis=-1, keepdims=True) + EPS)
    return values * factor * gain


def rope(values, cosine, sine):
    return values * cosine + pltpu.roll(values, HD // 2, 1) * sine


def norm_kernel(tokens, gain, out):
    out[...] = rms(tokens[...].astype(F32), gain[...]).astype(BF)


def kv_kernel(info, normed, key_weight, value_weight, gain, cosine, sine, own, other):
    plane = info[3]
    x = normed[...]
    keys = jnp.dot(x, key_weight[...], preferred_element_type=F32)
    vals = jnp.dot(x, value_weight[...], preferred_element_type=F32).astype(BF)
    cos, sin = cosine[0:ROWS], sine[0:ROWS]
    k0 = rope(rms(keys[:, :HD], gain[...]), cos, sin)
    k1 = rope(rms(keys[:, HD:], gain[...]), cos, sin)
    v0, v1 = vals[:, :HD].astype(F32), vals[:, HD:].astype(F32)
    first = plane == 0
    own[:, :HD] = jnp.where(first, k0, k1).astype(BF)
    own[:, HD:] = jnp.where(first, v0, v1).astype(BF)
    other[:, :HD] = jnp.where(first, k1, k0).astype(BF)
    other[:, HD:] = jnp.where(first, v1, v0).astype(BF)


def query_kernel(info, r0, r1, r2, r3, w_own, w_core, w_far, w_far_core, gain, cosine, sine, mine, far, x_s):
    core = info[4]
    for i, r in enumerate((r0, r1, r2, r3)):
        x_s[i * ROWS : (i + 1) * ROWS] = r[...]
    x = x_s[...]
    cos, sin = cosine[...], sine[...]
    scale = gain[...] * (LOG2E * HD**-0.5)
    for out, first, second in ((far, w_far, w_far_core), (mine, w_own, w_core)):
        q = jnp.dot(x, jnp.concatenate([first[...], second[...]], axis=1), preferred_element_type=F32)
        out[core] = rope(rms(q[:, :HD], scale), cos, sin).astype(BF)
        out[1 - core] = rope(rms(q[:, HD:], scale), cos, sin).astype(BF)


KEYS = 512


def attend_kernel(which, info, q, t0, t1, t2, t3, out, k_s, v_s, acc):
    ctx, me = info[0], info[1]
    base = jnp.bitwise_xor(me, which)
    y = jnp.bitwise_and(jnp.right_shift(me, 1), 3)
    for m, t in enumerate((t0, t1, t2, t3)):
        for i in range(4):
            source = jnp.bitwise_xor(ctx, 2 * m + (i >> 1) + 8 * (i & 1))
            at = pl.ds(pl.multiple_of(source * 128, 128), 128)
            k_s[at] = t[i, :, :HD]
            v_s[at, :HD] = t[i, :, HD:]
    v_s[:, HD:] = jnp.ones((16 * 128, HD), BF)
    out[:, :, 8 * HD :] = jnp.zeros((4, ROWS, 128), BF)
    last = ctx // (KEYS // 128)

    def scores(qv, chunk):
        at = pl.ds(pl.multiple_of(chunk * KEYS, KEYS), KEYS)
        s = lax.dot_general(qv, k_s[at], (((1,), (1,)), ((), ())), preferred_element_type=F32)
        return jnp.exp2(s), v_s[at]

    def per_piece(dd, carry):
        qv = q[dd].reshape(2 * 256, HD)
        key = lax.broadcasted_iota(jnp.int32, (2 * 256, KEYS), 1)
        row = lax.broadcasted_iota(jnp.int32, (2 * 256, 1), 0)
        key_dev = jnp.bitwise_xor(me, jnp.bitwise_and(jnp.right_shift(key, 6), 1) * 8)
        key_pos = (last * (KEYS // 128) + jnp.right_shift(key, 7)) * 1024 + key_dev * ROWS + jnp.bitwise_and(key, 63)
        row_dev = jnp.bitwise_xor(base, jnp.bitwise_xor(jnp.bitwise_and(jnp.right_shift(row, 6), 3), dd) * 2)
        row_pos = ctx * 1024 + row_dev * ROWS + jnp.bitwise_and(row, 63)
        w, v = scores(qv, last)
        w = jnp.where(key_pos <= row_pos, w, 0.0)
        acc[...] = jnp.dot(w.astype(BF), v, preferred_element_type=F32)

        def per_chunk(chunk, c):
            w, v = scores(qv, chunk)
            acc[...] += jnp.dot(w.astype(BF), v, preferred_element_type=F32)
            return c

        lax.fori_loop(0, last, per_chunk, 0)
        lane = lax.broadcasted_iota(jnp.int32, (ROWS, 128), 1)
        for p in range(2):
            head = jnp.bitwise_xor(y, dd) * 2 + p
            for i in range(4):
                rows = jnp.bitwise_xor(jnp.bitwise_xor(y, dd), i)
                block = acc[p * 256 + i * ROWS : p * 256 + (i + 1) * ROWS]
                out[rows, :, pl.ds(pl.multiple_of(head * HD, HD), HD)] = block[:, :HD].astype(BF)
                den = block[:, HD:]
                high = den.astype(BF)
                low = (den - high.astype(F32)).astype(BF)
                old = out[rows, :, 8 * HD :].astype(F32)
                new = jnp.where(lane == head, high.astype(F32), jnp.where(lane == head + 8, low.astype(F32), old))
                out[rows, :, 8 * HD :] = new.astype(BF)
        return carry

    lax.fori_loop(0, 4, per_piece, 0)


def fold_kernel(info, near, near_in, far, far_in, s0, s1, s2, s3):
    y, plane = info[2], info[3]
    for i, s in enumerate((s0, s1, s2, s3)):
        at = jnp.bitwise_xor(y, i)
        s[plane] = (near[at].astype(F32) + near_in[at].astype(F32)).astype(BF)
        s[1 - plane] = (far[at].astype(F32) + far_in[at].astype(F32)).astype(BF)


def project_kernel(info, s0, s1, s2, s3, weight, mine, far, x_s):
    plane = info[3]
    total = s0[...].astype(F32) + s1[...].astype(F32) + s2[...].astype(F32) + s3[...].astype(F32)
    total = total.reshape(2 * ROWS, WIDE)
    for h in range(8):
        den = total[:, 8 * HD + h : 8 * HD + h + 1] + total[:, 8 * HD + 8 + h : 8 * HD + 9 + h]
        x_s[:, h * HD : (h + 1) * HD] = (total[:, h * HD : (h + 1) * HD] / den).astype(BF)
    x = x_s[...]
    for n in range(4):
        cols = slice(n * 512, (n + 1) * 512)
        part = jnp.dot(x, weight[:, cols], preferred_element_type=F32)
        first = plane == 0
        mine[:, cols] = jnp.where(first, part[:ROWS], part[ROWS:])
        far[:, cols] = jnp.where(first, part[ROWS:], part[:ROWS]).astype(BF)


def hidden_kernel(tokens, part, part_in, gain, hidden, moe_in):
    h = (tokens[...].astype(F32) + (part[...] + part_in[...].astype(F32))).astype(BF)
    hidden[...] = h
    moe_in[...] = rms(h.astype(F32), gain[...]).astype(BF)


def expert_kernel(which, info, keep_in, swap_in, route, gate, up, down, keep, swap, x_s, acc):
    step = pl.program_id(0)
    me = info[1]

    @pl.when(step == 0)
    def _():
        x_s[: 4 * ROWS] = keep_in[...].reshape(4 * ROWS, D)
        x_s[4 * ROWS :] = swap_in[...].reshape(4 * ROWS, D)

    x = x_s[...]
    g = jnp.dot(x, gate[0], preferred_element_type=F32)
    u = jnp.dot(x, up[0], preferred_element_type=F32)
    inner = (g / (1.0 + jnp.exp(-g)) * u).astype(BF)
    part = jnp.dot(inner, down[0], preferred_element_type=F32)

    @pl.when(step == 0)
    def _():
        acc[...] = part

    @pl.when(step != 0)
    def _():
        acc[...] += part

    @pl.when(step == pl.num_programs(0) - 1)
    def _():
        lane = lax.broadcasted_iota(jnp.int32, (ROWS, 16), 1)
        for half, out in ((0, keep), (1, swap)):
            for i in range(4):
                owner = jnp.bitwise_xor(me, which + half + 2 * i)
                w = jnp.sum(jnp.where(lane == me, route[owner], 0.0), axis=1, keepdims=True)
                a = (half * 4 + i) * ROWS
                out[i] = (w * acc[a : a + ROWS].astype(BF).astype(F32)).astype(BF)


def expert(which, info, keep_in, swap_in, route, gate, up, down):
    tile = 256
    whole = lambda *shape: pl.BlockSpec(shape, lambda i: (0,) * len(shape))
    return pl.pallas_call(
        functools.partial(expert_kernel, which),
        grid=(FF // tile,),
        out_shape=[jax.ShapeDtypeStruct((4, ROWS, D), BF)] * 2,
        in_specs=[
            SM,
            whole(4, ROWS, D),
            whole(4, ROWS, D),
            whole(16, ROWS, 16),
            pl.BlockSpec((1, D, tile), lambda i: (0, 0, i)),
            pl.BlockSpec((1, D, tile), lambda i: (0, 0, i)),
            pl.BlockSpec((1, tile, D), lambda i: (0, i, 0)),
        ],
        out_specs=[whole(4, ROWS, D)] * 2,
        scratch_shapes=[pltpu.VMEM((8 * ROWS, D), BF), pltpu.VMEM((8 * ROWS, D), F32)],
        compiler_params=pltpu.CompilerParams(vmem_limit_bytes=48 * MB),
        cost_estimate=pl.CostEstimate(flops=8 * ROWS * D * FF * 6, bytes_accessed=14 * MB, transcendentals=0),
    )(info, keep_in, swap_in, route, gate, up, down)


def combine_kernel(keep, swap_in, s0, s1, s2, s3):
    for i, s in enumerate((s0, s1, s2, s3)):
        s[...] = (keep[i].astype(F32) + swap_in[i].astype(F32)).astype(s.dtype)


def total_kernel(s0, s1, s2, s3, out):
    out[...] = (s0[...] + s1[...].astype(F32) + s2[...].astype(F32) + s3[...].astype(F32)).astype(BF)


def final_kernel(hidden, s0, s1, s2, s3, far, out):
    mix = s0[...] + s1[...].astype(F32) + s2[...].astype(F32) + s3[...].astype(F32) + far[...].astype(F32)
    out[...] = (hidden[...].astype(F32) + mix).astype(BF)


def swap_exp(x, mask):
    return lax.ppermute(x, "exp", [(i, i ^ mask) for i in range(16)])


def swap_ctx(x, mask):
    return lax.ppermute(x, "ctx", [(i, i ^ mask) for i in range(16)])


def local(
    tokens,
    attn_gain,
    query_gain,
    key_gain,
    query_weight,
    key_weight,
    value_weight,
    out_weight,
    moe_gain,
    route_ids,
    route_weights,
    gate_weight,
    up_weight,
    down_weight,
):
    ctx = lax.axis_index("ctx").astype(jnp.int32)
    me = lax.axis_index("exp").astype(jnp.int32)
    y = (me >> 1) & 3
    info = jnp.stack([ctx, me, y, me >> 3, me & 1])
    planes = [list(range(8)), list(range(8, 16))]

    w_out = lax.all_gather(out_weight, "exp", axis=0, tiled=True, axis_index_groups=planes)
    chosen = route_ids[:, :, None] == jnp.arange(16, dtype=jnp.int32)
    route = jnp.sum(jnp.where(chosen, route_weights[:, :, None], 0.0), axis=1)
    route = lax.all_gather(route, "exp", axis=0, tiled=False)

    exponent = jnp.arange(HD // 2, dtype=F32) * (2.0 / HD)
    inverse = jnp.power(jnp.float32(ROPE_BASE), -exponent)
    owners = me ^ (2 * jnp.arange(4, dtype=jnp.int32))
    positions = (ctx * 1024 + owners[:, None] * ROWS + jnp.arange(ROWS, dtype=jnp.int32)[None, :]).reshape(-1)
    angles = positions.astype(F32)[:, None] * inverse[None, :]
    cosine, sine = jnp.cos(angles), jnp.sin(angles)
    cosine = jnp.concatenate([cosine, cosine], axis=1)
    sine = jnp.concatenate([-sine, sine], axis=1)

    w_far = swap_exp(query_weight, 8)
    w_core = swap_exp(query_weight, 1)
    [normed] = call(norm_kernel, (tokens, attn_gain[None]), [((ROWS, D), BF)], scalars=False, moved=MB)
    near = [swap_exp(normed, 2 * i) for i in (1, 2, 3)]
    own, other = call(
        kv_kernel,
        (info, normed, key_weight, value_weight, key_gain[None], cosine, sine),
        [((ROWS, 2 * HD), BF)] * 2,
        flops=ROWS * D * 1024,
        moved=2 * MB,
    )
    w_far_core = swap_exp(w_far, 1)
    other = swap_exp(other, 8)
    pair = jnp.concatenate([own, other], axis=0)
    pair = jnp.stack([pair, swap_ctx(pair, 8)])
    quad = jnp.concatenate([pair, swap_ctx(pair, 1)], axis=0)
    keys = [quad] + [swap_ctx(quad, 2 * i) for i in (1, 2, 3)]

    mine, far = call(
        query_kernel,
        (info, normed, *near, query_weight, w_core, w_far, w_far_core, query_gain[None], cosine, sine),
        [((2, 256, HD), BF)] * 2,
        flops=256 * D * 1024,
        moved=4 * MB,
        scratch=[pltpu.VMEM((256, D), BF)],
    )
    far = swap_exp(far, 8)
    q_near = jnp.stack([mine] + [swap_exp(mine, 2 * i) for i in (1, 2, 3)])
    q_far = jnp.stack([far] + [swap_exp(far, 2 * i) for i in (1, 2, 3)])
    q_near_core = swap_exp(q_near, 1)
    q_far_core = swap_exp(q_far, 1)

    def attend(which, q):
        return call(
            functools.partial(attend_kernel, which),
            (info, q, *keys),
            [((4, ROWS, WIDE), BF)],
            flops=2048 * 2048 * 512,
            moved=3 * MB,
            scratch=[
                pltpu.VMEM((2048, HD), BF),
                pltpu.VMEM((2048, 2 * HD), BF),
                pltpu.VMEM((512, 2 * HD), F32),
            ],
        )[0]

    a_near, a_far = attend(0, q_near), attend(8, q_far)
    a_near_core, a_far_core = attend(1, q_near_core), attend(9, q_far_core)
    near_in, far_in = swap_exp(a_near_core, 1), swap_exp(a_far_core, 1)
    parts = call(fold_kernel, (info, a_near, near_in, a_far, far_in), [((2, ROWS, WIDE), BF)] * 4, moved=5 * MB)
    parts = [parts[0]] + [swap_exp(parts[i], 2 * i) for i in (1, 2, 3)]
    part, part_far = call(
        project_kernel,
        (info, *parts, w_out),
        [((ROWS, D), F32), ((ROWS, D), BF)],
        flops=128 * 1024 * 2048 * 2,
        moved=6 * MB,
        scratch=[pltpu.VMEM((2 * ROWS, 8 * HD), BF)],
    )
    part_in = swap_exp(part_far, 8)
    hidden, moe_in = call(
        hidden_kernel, (tokens, part, part_in, moe_gain[None]), [((ROWS, D), BF)] * 2, scalars=False, moved=2 * MB
    )

    moe_far = swap_exp(moe_in, 8)
    m_near = jnp.stack([moe_in] + [swap_exp(moe_in, 2 * i) for i in (1, 2, 3)])
    m_far = jnp.stack([moe_far] + [swap_exp(moe_far, 2 * i) for i in (1, 2, 3)])
    m_near_core, m_far_core = swap_exp(m_near, 1), swap_exp(m_far, 1)

    def run_expert(which, keep_in, swap_in):
        keep, swap = expert(which, info, keep_in, swap_in, route, gate_weight, up_weight, down_weight)
        swap_back = swap_exp(swap, 1)
        s = call(
            combine_kernel,
            (keep, swap_back),
            [((ROWS, D), F32)] + [((ROWS, D), BF)] * 3,
            scalars=False,
            moved=4 * MB,
        )
        return [s[0]] + [swap_exp(s[i], 2 * i) for i in (1, 2, 3)]

    s_near = run_expert(0, m_near, m_near_core)
    s_far = run_expert(8, m_far, m_far_core)
    [out_far] = call(total_kernel, tuple(s_far), [((ROWS, D), BF)], scalars=False, moved=2 * MB)
    [out] = call(
        final_kernel, (hidden, *s_near, swap_exp(out_far, 8)), [((ROWS, D), BF)], scalars=False, moved=2 * MB
    )
    return out


def solution(mesh):
    rows = P(("ctx", "exp"), None)
    return jax.shard_map(
        local,
        mesh=mesh,
        in_specs=(
            rows,
            P(),
            P(),
            P(),
            P(None, "exp"),
            P(),
            P(),
            P("exp", None),
            P(),
            rows,
            rows,
            P("exp", None, None),
            P("exp", None, None),
            P("exp", None, None),
        ),
        out_specs=rows,
        check_vma=False,
    )
```

```python
import functools

import jax
import jax.numpy as jnp
from jax import lax
from jax.experimental import pallas as pl
from jax.experimental.pallas import tpu as pltpu
from jax.sharding import PartitionSpec as P

EPS = 1e-06
ROPE_BASE = 1000000.0
HD = 128
D = 2048
FF = 768
ROWS = 64
WIDE = 8 * HD + 128
LOG2E = 1.4426950408889634
MB = 1 << 20
BF = jnp.bfloat16
F32 = jnp.float32

VM = pl.BlockSpec(memory_space=pltpu.VMEM)
SM = pl.BlockSpec(memory_space=pltpu.SMEM)
ANY = pl.BlockSpec(memory_space=pl.ANY)
HBM = pl.BlockSpec(memory_space=pltpu.HBM)


def call(kernel, args, outs, flops=0, moved=0, scratch=(), scalars=True, limit=16, in_hbm=(), hbm=ANY):
    specs = [hbm if i in in_hbm else SM if scalars and i == 0 else VM for i in range(len(args))]
    return pl.pallas_call(
        kernel,
        out_shape=[jax.ShapeDtypeStruct(s, t) for s, t in outs],
        in_specs=specs,
        out_specs=[VM] * len(outs),
        scratch_shapes=list(scratch),
        compiler_params=pltpu.CompilerParams(vmem_limit_bytes=limit * MB),
        cost_estimate=pl.CostEstimate(flops=flops, bytes_accessed=moved, transcendentals=0),
    )(*args)


def rms(values, gain):
    factor = lax.rsqrt(jnp.mean(values * values, axis=-1, keepdims=True) + EPS)
    return values * factor * gain


def rope(values, cosine, sine):
    return values * cosine + pltpu.roll(values, HD // 2, 1) * sine


def norm_kernel(tokens, gain, out):
    out[...] = rms(tokens[...].astype(F32), gain[...]).astype(BF)


def kv_kernel(info, normed, key_weight, value_weight, gain, cosine, sine, own, other, kw, vw, sems):
    plane = info[3]
    loads = [pltpu.make_async_copy(key_weight, kw, sems.at[0]), pltpu.make_async_copy(value_weight, vw, sems.at[1])]
    for load in loads:
        load.start()
    x = normed[...]
    loads[0].wait()
    keys = jnp.dot(x, kw[...], preferred_element_type=F32)
    loads[1].wait()
    vals = jnp.dot(x, vw[...], preferred_element_type=F32).astype(BF)
    cos, sin = cosine[0:ROWS], sine[0:ROWS]
    k0 = rope(rms(keys[:, :HD], gain[...]), cos, sin)
    k1 = rope(rms(keys[:, HD:], gain[...]), cos, sin)
    v0, v1 = vals[:, :HD].astype(F32), vals[:, HD:].astype(F32)
    first = plane == 0
    own[:, :HD] = jnp.where(first, k0, k1).astype(BF)
    own[:, HD:] = jnp.where(first, v0, v1).astype(BF)
    other[:, :HD] = jnp.where(first, k1, k0).astype(BF)
    other[:, HD:] = jnp.where(first, v1, v0).astype(BF)


def query_kernel(info, r0, r1, r2, r3, w_own, w_core, w_far, w_far_core, gain, cosine, sine, mine, far, x_s):
    core = info[4]
    for i, r in enumerate((r0, r1, r2, r3)):
        x_s[i * ROWS : (i + 1) * ROWS] = r[...]
    x = x_s[...]
    cos, sin = cosine[...], sine[...]
    scale = gain[...] * (LOG2E * HD**-0.5)
    for out, first, second in ((far, w_far, w_far_core), (mine, w_own, w_core)):
        q = jnp.dot(x, jnp.concatenate([first[...], second[...]], axis=1), preferred_element_type=F32)
        out[core] = rope(rms(q[:, :HD], scale), cos, sin).astype(BF)
        out[1 - core] = rope(rms(q[:, HD:], scale), cos, sin).astype(BF)


KEYS = 512


def attend_kernel(which, info, q, t0, t1, t2, t3, out, k_s, v_s, acc):
    ctx, me = info[0], info[1]
    base = jnp.bitwise_xor(me, which)
    y = jnp.bitwise_and(jnp.right_shift(me, 1), 3)
    for m, t in enumerate((t0, t1, t2, t3)):
        for i in range(4):
            valid = jnp.bitwise_xor(ctx, 2 * m + (i >> 1) + 8 * (i & 1)) <= ctx
            at = slice((4 * m + i) * 128, (4 * m + i + 1) * 128)
            k_s[at] = t[i, :, :HD]
            v_s[at, :HD] = jnp.where(valid, t[i, :, HD:].astype(F32), 0.0).astype(BF)
            v_s[at, HD:] = jnp.full((128, HD), jnp.where(valid, 1.0, 0.0), F32).astype(BF)
    out[:, :, 8 * HD :] = jnp.zeros((4, ROWS, 128), BF)
    lane = lax.broadcasted_iota(jnp.int32, (ROWS, 128), 1)

    def per_piece(dd, carry):
        row = lax.broadcasted_iota(jnp.int32, (256, 1), 0)
        key = lax.broadcasted_iota(jnp.int32, (256, 128), 1)
        key_dev = jnp.bitwise_xor(me, jnp.bitwise_and(jnp.right_shift(key, 6), 1) * 8)
        row_dev = jnp.bitwise_xor(base, jnp.bitwise_xor(jnp.right_shift(row, 6), dd) * 2)
        allowed = key_dev * ROWS + jnp.bitwise_and(key, 63) <= row_dev * ROWS + jnp.bitwise_and(row, 63)
        for p in range(2):
            qv = q[dd, which >> 3, p]
            total = None
            for c in range(0, 2048, KEYS):
                s = lax.dot_general(
                    qv, k_s[c : c + KEYS], (((1,), (1,)), ((), ())), preferred_element_type=F32
                )
                w = jnp.exp2(s)
                if c == 0:
                    w = jnp.concatenate([jnp.where(allowed, w[:, :128], 0.0), w[:, 128:]], axis=1)
                o = jnp.dot(w.astype(BF), v_s[c : c + KEYS], preferred_element_type=F32)
                total = o if total is None else total + o
            acc[p * 256 : (p + 1) * 256] = total
        for p in range(2):
            head = jnp.bitwise_xor(y, dd) * 2 + p
            for i in range(4):
                rows = jnp.bitwise_xor(jnp.bitwise_xor(y, dd), i)
                block = acc[p * 256 + i * ROWS : p * 256 + (i + 1) * ROWS]
                out[rows, :, pl.ds(pl.multiple_of(head * HD, HD), HD)] = block[:, :HD].astype(BF)
                den = block[:, HD:]
                high = den.astype(BF).astype(F32)
                old = out[rows, :, 8 * HD :].astype(F32)
                new = jnp.where(lane == head, high, jnp.where(lane == head + 8, den - high, old))
                out[rows, :, 8 * HD :] = new.astype(BF)
        return carry

    lax.fori_loop(0, 4, per_piece, 0, unroll=True)


def fold_kernel(info, part, part_in, s0, s1, s2, s3):
    y = info[2]
    for i, s in enumerate((s0, s1, s2, s3)):
        at = jnp.bitwise_xor(y, i)
        s[...] = (part[at].astype(F32) + part_in[at].astype(F32)).astype(BF)


def project_kernel(s0, s1, s2, s3, weight, out, x_s, w_s, sems):
    cols = [slice(n * 512, (n + 1) * 512) for n in range(4)]
    loads = [pltpu.make_async_copy(weight.at[:, c], w_s.at[:, c], sems.at[n]) for n, c in enumerate(cols)]
    for load in loads:
        load.start()
    total = s0[...].astype(F32) + s1[...].astype(F32) + s2[...].astype(F32) + s3[...].astype(F32)
    for h in range(8):
        den = total[:, 8 * HD + h : 8 * HD + h + 1] + total[:, 8 * HD + 8 + h : 8 * HD + 9 + h]
        x_s[:, h * HD : (h + 1) * HD] = (total[:, h * HD : (h + 1) * HD] / den).astype(BF)
    x = x_s[...]
    for c, load in zip(cols, loads):
        load.wait()
        out[:, c] = jnp.dot(x, w_s[:, c], preferred_element_type=F32).astype(out.dtype)


def project(parts, weight, kind):
    return call(
        project_kernel,
        (*parts, weight),
        [((ROWS, D), kind)],
        scalars=False,
        in_hbm=(4,),
        hbm=HBM,
        flops=ROWS * 2048 * 2048,
        moved=5 * MB,
        scratch=[pltpu.VMEM((ROWS, 8 * HD), BF), pltpu.VMEM((8 * HD, D), BF), pltpu.SemaphoreType.DMA((4,))],
    )[0]


def route_kernel(ids, weights, out):
    lane = lax.broadcasted_iota(jnp.int32, (ROWS, 128), 1)
    table = jnp.zeros((ROWS, 128), F32)
    for k in range(8):
        expert, weight = ids[:, k : k + 1], weights[:, k : k + 1]
        high = weight.astype(BF).astype(F32)
        table = jnp.where(lane == expert, high, jnp.where(lane == expert + 16, weight - high, table))
    out[...] = table.astype(BF)


def hidden_kernel(tokens, part, part_in, gain, route, hidden, moe_in):
    h = (tokens[...].astype(F32) + (part[...] + part_in[...].astype(F32))).astype(BF)
    hidden[...] = h
    moe_in[:, :D] = rms(h.astype(F32), gain[...]).astype(BF)
    moe_in[:, D:] = route[...]


def expert_kernel(info, keep_in, swap_in, gate, up, down, keep, swap, x_s, inner_s, w_s, gate_s, up_s, down_s, sems):
    me = info[1]
    cols = [slice(n * 256, (n + 1) * 256) for n in range(FF // 256)]
    loads = []
    for n, c in enumerate(cols):
        loads.append(pltpu.make_async_copy(gate.at[0, :, c], gate_s.at[:, c], sems.at[2 * n]))
        loads.append(pltpu.make_async_copy(up.at[0, :, c], up_s.at[:, c], sems.at[2 * n + 1]))
    loads.append(pltpu.make_async_copy(down.at[0], down_s, sems.at[6]))
    for load in loads:
        load.start()
    lane = lax.broadcasted_iota(jnp.int32, (4 * ROWS, 128), 1)
    for rows, at in ((swap_in, slice(0, 4 * ROWS)), (keep_in, slice(4 * ROWS, 8 * ROWS))):
        both = rows[...].reshape(4 * ROWS, D + 128)
        x_s[at] = both[:, :D]
        w = jnp.where((lane == me) | (lane == me + 16), both[:, D:].astype(F32), 0.0)
        w_s[at] = jnp.broadcast_to(jnp.sum(w, axis=1, keepdims=True), (4 * ROWS, 128))
    x = x_s[...]
    for n, c in enumerate(cols):
        loads[2 * n].wait()
        g = jnp.dot(x, gate_s[:, c], preferred_element_type=F32)
        loads[2 * n + 1].wait()
        u = jnp.dot(x, up_s[:, c], preferred_element_type=F32)
        inner_s[:, c] = (g / (1.0 + jnp.exp(-g)) * u).astype(BF)
    loads[6].wait()
    inner = inner_s[...]
    for n in range(8):
        c = slice(n * 256, (n + 1) * 256)
        res = jnp.dot(inner, down_s[:, c], preferred_element_type=F32).astype(BF).astype(F32)
        w = w_s[...]
        res = (jnp.concatenate([w, w], axis=1) * res).astype(BF)
        swap[:, :, c] = res[: 4 * ROWS].reshape(4, ROWS, 256)
        keep[:, :, c] = res[4 * ROWS :].reshape(4, ROWS, 256)


def combine_kernel(keep, swap_in, s0, s1, s2, s3):
    for i, s in enumerate((s0, s1, s2, s3)):
        s[...] = (keep[i].astype(F32) + swap_in[i].astype(F32)).astype(s.dtype)


def total_kernel(s0, s1, s2, s3, out):
    out[...] = (s0[...] + s1[...].astype(F32) + s2[...].astype(F32) + s3[...].astype(F32)).astype(BF)


def final_kernel(hidden, s0, s1, s2, s3, far, out):
    mix = s0[...] + s1[...].astype(F32) + s2[...].astype(F32) + s3[...].astype(F32) + far[...].astype(F32)
    out[...] = (hidden[...].astype(F32) + mix).astype(BF)


def after(x, y):
    return lax.optimization_barrier((x, y))[0]


def swap_exp(x, mask):
    return lax.ppermute(x, "exp", [(i, i ^ mask) for i in range(16)])


def swap_ctx(x, mask):
    return lax.ppermute(x, "ctx", [(i, i ^ mask) for i in range(16)])


def local(
    tokens,
    attn_gain,
    query_gain,
    key_gain,
    query_weight,
    key_weight,
    value_weight,
    out_weight,
    moe_gain,
    route_ids,
    route_weights,
    gate_weight,
    up_weight,
    down_weight,
):
    ctx = lax.axis_index("ctx").astype(jnp.int32)
    me = lax.axis_index("exp").astype(jnp.int32)
    y = (me >> 1) & 3
    info = jnp.stack([ctx, me, y, me >> 3, me & 1])
    planes = [list(range(8)), list(range(8, 16))]

    w_out = lax.all_gather(out_weight, "exp", axis=0, tiled=True, axis_index_groups=planes)
    [route] = call(route_kernel, (route_ids, route_weights), [((ROWS, 128), BF)], scalars=False)

    exponent = jnp.arange(HD // 2, dtype=F32) * (2.0 / HD)
    inverse = jnp.power(jnp.float32(ROPE_BASE), -exponent)
    owners = me ^ (2 * jnp.arange(4, dtype=jnp.int32))
    positions = (ctx * 1024 + owners[:, None] * ROWS + jnp.arange(ROWS, dtype=jnp.int32)[None, :]).reshape(-1)
    angles = positions.astype(F32)[:, None] * inverse[None, :]
    cosine, sine = jnp.cos(angles), jnp.sin(angles)
    cosine = jnp.concatenate([cosine, cosine], axis=1)
    sine = jnp.concatenate([-sine, sine], axis=1)

    w_far = swap_exp(query_weight, 8)
    w_core = swap_exp(query_weight, 1)
    [normed] = call(norm_kernel, (tokens, attn_gain[None]), [((ROWS, D), BF)], scalars=False, moved=MB)
    near = [swap_exp(normed, 2 * i) for i in (1, 2, 3)]
    own, other = call(
        kv_kernel,
        (info, normed, key_weight, value_weight, key_gain[None], cosine, sine),
        [((ROWS, 2 * HD), BF)] * 2,
        flops=ROWS * D * 1024,
        moved=2 * MB,
        in_hbm=(2, 3),
        scratch=[pltpu.VMEM((D, 2 * HD), BF), pltpu.VMEM((D, 2 * HD), BF), pltpu.SemaphoreType.DMA((2,))],
    )
    other = swap_exp(other, 8)
    w_far = after(w_far, (near, other))
    w_far_core = swap_exp(w_far, 1)
    pair = jnp.concatenate([own, other], axis=0)
    pair_in = swap_ctx(pair, 8)
    pair = jnp.stack([pair, pair_in])
    quad = jnp.concatenate([pair, swap_ctx(pair, 1)], axis=0)
    keys = [quad] + [swap_ctx(quad, 2 * i) for i in (1, 2, 3)]

    mine, far = call(
        query_kernel,
        (info, normed, *near, query_weight, w_core, w_far, w_far_core, query_gain[None], cosine, sine),
        [((2, 256, HD), BF)] * 2,
        flops=256 * D * 1024,
        moved=4 * MB,
        scratch=[pltpu.VMEM((256, D), BF)],
    )
    far = swap_exp(after(far, pair_in), 8)
    both = jnp.stack([mine, after(far, quad)])
    queries = jnp.stack([both] + [swap_exp(both, 2 * i) for i in (1, 2, 3)])
    queries_core = swap_exp(after(queries, keys), 1)

    def attend(which, q):
        return call(
            functools.partial(attend_kernel, which),
            (info, q, *keys),
            [((4, ROWS, WIDE), BF)],
            flops=2048 * 2048 * 512,
            moved=3 * MB,
            scratch=[
                pltpu.VMEM((2048, HD), BF),
                pltpu.VMEM((2048, 2 * HD), BF),
                pltpu.VMEM((512, 2 * HD), F32),
            ],
        )[0]

    def fold(part, part_core):
        parts = call(
            fold_kernel, (info, part, swap_exp(part_core, 1)), [((ROWS, WIDE), BF)] * 4, moved=2 * MB
        )
        return [parts[0]] + [swap_exp(parts[i], 2 * i) for i in (1, 2, 3)]

    a_far = attend(8, queries)
    a_far_core = attend(9, after(queries_core, a_far))
    a_near_core = attend(1, after(queries_core, a_far_core))
    a_near = attend(0, after(queries, (a_near_core, w_out)))
    sums_far, sums_near = fold(a_far, a_far_core), fold(a_near, a_near_core)
    part_in = swap_exp(project(after(sums_far, sums_near[0]), w_out, BF), 8)
    part = project(sums_near, w_out, F32)
    hidden, moe_in = call(
        hidden_kernel,
        (tokens, part, part_in, moe_gain[None], route),
        [((ROWS, D), BF), ((ROWS, D + 128), BF)],
        scalars=False,
        moved=2 * MB,
    )

    moe_far = swap_exp(moe_in, 8)
    m_near = [moe_in] + [swap_exp(moe_in, 2 * i) for i in (1, 2, 3)]
    moe_far = after(moe_far, (m_near[1], m_near[3]))
    m_far = jnp.stack([moe_far] + [swap_exp(moe_far, 2 * i) for i in (1, 2, 3)])
    m_near = jnp.stack(m_near)
    m_near_core, m_far_core = swap_exp(m_near, 1), swap_exp(m_far, 1)

    def run_expert(keep_in, swap_in):
        keep, swap = call(
            expert_kernel,
            (info, keep_in, swap_in, gate_weight, up_weight, down_weight),
            [((4, ROWS, D), BF)] * 2,
            flops=8 * ROWS * D * FF * 6,
            moved=14 * MB,
            in_hbm=(3, 4, 5),
            limit=28,
            scratch=[
                pltpu.VMEM((8 * ROWS, D), BF),
                pltpu.VMEM((8 * ROWS, FF), BF),
                pltpu.VMEM((8 * ROWS, 128), F32),
                pltpu.VMEM((D, FF), BF),
                pltpu.VMEM((D, FF), BF),
                pltpu.VMEM((FF, D), BF),
                pltpu.SemaphoreType.DMA((7,)),
            ],
        )
        swap_back = swap_exp(swap, 1)
        s = call(
            combine_kernel,
            (keep, swap_back),
            [((ROWS, D), F32)] + [((ROWS, D), BF)] * 3,
            scalars=False,
            moved=4 * MB,
        )
        return [s[0]] + [swap_exp(s[i], 2 * i) for i in (1, 2, 3)]

    s_near = run_expert(m_near, m_near_core)
    s_far = run_expert(m_far, m_far_core)
    [out_far] = call(total_kernel, tuple(s_far), [((ROWS, D), BF)], scalars=False, moved=2 * MB)
    [out] = call(
        final_kernel, (hidden, *s_near, swap_exp(out_far, 8)), [((ROWS, D), BF)], scalars=False, moved=2 * MB
    )
    return out


def solution(mesh):
    rows = P(("ctx", "exp"), None)
    return jax.shard_map(
        local,
        mesh=mesh,
        in_specs=(
            rows,
            P(),
            P(),
            P(),
            P(None, "exp"),
            P(),
            P(),
            P("exp", None),
            P(),
            rows,
            rows,
            P("exp", None, None),
            P("exp", None, None),
            P("exp", None, None),
        ),
        out_specs=rows,
        check_vma=False,
    )
```

```python
import functools

import jax
import jax.numpy as jnp
from jax import lax
from jax.experimental import pallas as pl
from jax.experimental.pallas import tpu as pltpu
from jax.sharding import PartitionSpec as P

EPS = 1e-06
ROPE_BASE = 1000000.0
HD = 128
D = 2048
FF = 768
ROWS = 64
WIDE = 8 * HD + 128
LOG2E = 1.4426950408889634
MB = 1 << 20
BF = jnp.bfloat16
F32 = jnp.float32

VM = pl.BlockSpec(memory_space=pltpu.VMEM)
SM = pl.BlockSpec(memory_space=pltpu.SMEM)
ANY = pl.BlockSpec(memory_space=pl.ANY)
HBM = pl.BlockSpec(memory_space=pltpu.HBM)


def call(kernel, args, outs, flops=0, moved=0, scratch=(), scalars=True, limit=12, in_hbm=(), hbm=ANY):
    specs = [hbm if i in in_hbm else SM if scalars and i == 0 else VM for i in range(len(args))]
    return pl.pallas_call(
        kernel,
        out_shape=[jax.ShapeDtypeStruct(s, t) for s, t in outs],
        in_specs=specs,
        out_specs=[VM] * len(outs),
        scratch_shapes=list(scratch),
        compiler_params=pltpu.CompilerParams(vmem_limit_bytes=limit * MB),
        cost_estimate=pl.CostEstimate(flops=flops, bytes_accessed=moved, transcendentals=0),
    )(*args)


def rms(values, gain):
    factor = lax.rsqrt(jnp.mean(values * values, axis=-1, keepdims=True) + EPS)
    return values * factor * gain


def rope(values, cosine, sine):
    return values * cosine + pltpu.roll(values, HD // 2, 1) * sine


def norm_kernel(tokens, gain, out):
    out[...] = rms(tokens[...].astype(F32), gain[...]).astype(BF)


def kv_kernel(info, normed, key_weight, value_weight, gain, cosine, sine, own, other, kw, vw, sems):
    plane = info[3]
    loads = [pltpu.make_async_copy(key_weight, kw, sems.at[0]), pltpu.make_async_copy(value_weight, vw, sems.at[1])]
    for load in loads:
        load.start()
    x = normed[...]
    loads[0].wait()
    keys = jnp.dot(x, kw[...], preferred_element_type=F32)
    loads[1].wait()
    vals = jnp.dot(x, vw[...], preferred_element_type=F32).astype(BF)
    cos, sin = cosine[0:ROWS], sine[0:ROWS]
    k0 = rope(rms(keys[:, :HD], gain[...]), cos, sin)
    k1 = rope(rms(keys[:, HD:], gain[...]), cos, sin)
    v0, v1 = vals[:, :HD].astype(F32), vals[:, HD:].astype(F32)
    first = plane == 0
    own[:, :HD] = jnp.where(first, k0, k1).astype(BF)
    own[:, HD:] = jnp.where(first, v0, v1).astype(BF)
    other[:, :HD] = jnp.where(first, k1, k0).astype(BF)
    other[:, HD:] = jnp.where(first, v1, v0).astype(BF)


def query_kernel(info, r0, r1, r2, r3, w_own, w_core, w_far, w_far_core, gain, cosine, sine, mine, far, x_s):
    core = info[4]
    for i, r in enumerate((r0, r1, r2, r3)):
        x_s[i * ROWS : (i + 1) * ROWS] = r[...]
    x = x_s[...]
    cos, sin = cosine[...], sine[...]
    scale = gain[...] * (LOG2E * HD**-0.5)
    for out, first, second in ((far, w_far, w_far_core), (mine, w_own, w_core)):
        q = jnp.dot(x, jnp.concatenate([first[...], second[...]], axis=1), preferred_element_type=F32)
        out[core] = rope(rms(q[:, :HD], scale), cos, sin).astype(BF)
        out[1 - core] = rope(rms(q[:, HD:], scale), cos, sin).astype(BF)


KEYS = 512


def attend_kernel(which, info, q, t0, t1, t2, t3, t4, out, k_s, v_s, acc):
    ctx, me = info[0], info[1]
    base = jnp.bitwise_xor(me, which)
    y = jnp.bitwise_and(jnp.right_shift(me, 1), 3)
    at = 0
    for t, distance in ((t0, (0, 4)), (t1, (-1, 3)), (t2, (1, 5)), (t3, (-2,)), (t4, (2,))):
        for j, d in enumerate(distance):
            for i in range(2):
                z = jnp.bitwise_and(ctx + (8 + d), 7)
                source = jnp.bitwise_and(jnp.bitwise_xor(ctx, 8 * i), 8) + z
                valid = source <= ctx
                k_s[at : at + 128] = t[j, i, :, :HD]
                v_s[at : at + 128, :HD] = jnp.where(valid, t[j, i, :, HD:].astype(F32), 0.0).astype(BF)
                v_s[at : at + 128, HD:] = jnp.full((128, HD), jnp.where(valid, 1.0, 0.0), F32).astype(BF)
                at += 128
    out[:, :, 8 * HD :] = jnp.zeros((4, ROWS, 128), BF)
    lane = lax.broadcasted_iota(jnp.int32, (ROWS, 128), 1)

    def per_piece(dd, carry):
        row = lax.broadcasted_iota(jnp.int32, (256, 1), 0)
        key = lax.broadcasted_iota(jnp.int32, (256, 128), 1)
        key_dev = jnp.bitwise_xor(me, jnp.bitwise_and(jnp.right_shift(key, 6), 1) * 8)
        row_dev = jnp.bitwise_xor(base, jnp.bitwise_xor(jnp.right_shift(row, 6), dd) * 2)
        allowed = key_dev * ROWS + jnp.bitwise_and(key, 63) <= row_dev * ROWS + jnp.bitwise_and(row, 63)
        for p in range(2):
            qv = q[dd, which >> 3, p]
            total = None
            for c in range(0, 2048, KEYS):
                s = lax.dot_general(
                    qv, k_s[c : c + KEYS], (((1,), (1,)), ((), ())), preferred_element_type=F32
                )
                w = jnp.exp2(s)
                if c == 0:
                    w = jnp.concatenate([jnp.where(allowed, w[:, :128], 0.0), w[:, 128:]], axis=1)
                o = jnp.dot(w.astype(BF), v_s[c : c + KEYS], preferred_element_type=F32)
                total = o if total is None else total + o
            acc[p * 256 : (p + 1) * 256] = total
        for p in range(2):
            head = jnp.bitwise_xor(y, dd) * 2 + p
            for i in range(4):
                rows = jnp.bitwise_xor(jnp.bitwise_xor(y, dd), i)
                block = acc[p * 256 + i * ROWS : p * 256 + (i + 1) * ROWS]
                out[rows, :, pl.ds(pl.multiple_of(head * HD, HD), HD)] = block[:, :HD].astype(BF)
                den = block[:, HD:]
                high = den.astype(BF).astype(F32)
                old = out[rows, :, 8 * HD :].astype(F32)
                new = jnp.where(lane == head, high, jnp.where(lane == head + 8, den - high, old))
                out[rows, :, 8 * HD :] = new.astype(BF)
        return carry

    lax.fori_loop(0, 4, per_piece, 0, unroll=True)


def fold_kernel(info, part, part_in, s0, s1, s2, s3):
    y = info[2]
    for i, s in enumerate((s0, s1, s2, s3)):
        at = jnp.bitwise_xor(y, i)
        s[...] = (part[at].astype(F32) + part_in[at].astype(F32)).astype(BF)


def project_kernel(s0, s1, s2, s3, weight, out, x_s, w_s, sems):
    cols = [slice(n * 512, (n + 1) * 512) for n in range(4)]
    loads = [pltpu.make_async_copy(weight.at[:, c], w_s.at[:, c], sems.at[n]) for n, c in enumerate(cols)]
    for load in loads:
        load.start()
    total = s0[...].astype(F32) + s1[...].astype(F32) + s2[...].astype(F32) + s3[...].astype(F32)
    for h in range(8):
        den = total[:, 8 * HD + h : 8 * HD + h + 1] + total[:, 8 * HD + 8 + h : 8 * HD + 9 + h]
        x_s[:, h * HD : (h + 1) * HD] = (total[:, h * HD : (h + 1) * HD] / den).astype(BF)
    x = x_s[...]
    for c, load in zip(cols, loads):
        load.wait()
        out[:, c] = jnp.dot(x, w_s[:, c], preferred_element_type=F32).astype(out.dtype)


def project(parts, weight, kind):
    return call(
        project_kernel,
        (*parts, weight),
        [((ROWS, D), kind)],
        scalars=False,
        in_hbm=(4,),
        hbm=HBM,
        flops=ROWS * 2048 * 2048,
        moved=5 * MB,
        scratch=[pltpu.VMEM((ROWS, 8 * HD), BF), pltpu.VMEM((8 * HD, D), BF), pltpu.SemaphoreType.DMA((4,))],
    )[0]


def route_kernel(ids, weights, out):
    lane = lax.broadcasted_iota(jnp.int32, (ROWS, 128), 1)
    table = jnp.zeros((ROWS, 128), F32)
    for k in range(8):
        expert, weight = ids[:, k : k + 1], weights[:, k : k + 1]
        high = weight.astype(BF).astype(F32)
        table = jnp.where(lane == expert, high, jnp.where(lane == expert + 16, weight - high, table))
    out[...] = table.astype(BF)


def hidden_kernel(tokens, part, part_in, gain, route, hidden, moe_in):
    h = (tokens[...].astype(F32) + (part[...] + part_in[...].astype(F32))).astype(BF)
    hidden[...] = h
    moe_in[:, :D] = rms(h.astype(F32), gain[...]).astype(BF)
    moe_in[:, D:] = route[...]


def expert_kernel(info, rows, gate, up, down, out, inner_s):
    me = info[1]
    lane = lax.broadcasted_iota(jnp.int32, (4 * ROWS, 128), 1)
    both = rows[...].reshape(4 * ROWS, D + 128)
    x = both[:, :D]
    w = jnp.where((lane == me) | (lane == me + 16), both[:, D:].astype(F32), 0.0)
    w = jnp.broadcast_to(jnp.sum(w, axis=1, keepdims=True), (4 * ROWS, 256))
    for n in range(FF // 256):
        c = slice(n * 256, (n + 1) * 256)
        g = jnp.dot(x, gate[0, :, c], preferred_element_type=F32)
        u = jnp.dot(x, up[0, :, c], preferred_element_type=F32)
        inner_s[:, c] = (g / (1.0 + jnp.exp(-g)) * u).astype(BF)
    inner = inner_s[...]
    for n in range(D // 256):
        c = slice(n * 256, (n + 1) * 256)
        res = jnp.dot(inner, down[0, :, c], preferred_element_type=F32).astype(BF).astype(F32)
        out[:, :, c] = (w * res).astype(BF).reshape(4, ROWS, 256)


def combine_kernel(keep, swap_in, s0, s1, s2, s3):
    for i, s in enumerate((s0, s1, s2, s3)):
        s[...] = (keep[i].astype(F32) + swap_in[i].astype(F32)).astype(s.dtype)


def total_kernel(s0, s1, s2, s3, out):
    out[...] = (s0[...] + s1[...].astype(F32) + s2[...].astype(F32) + s3[...].astype(F32)).astype(BF)


def final_kernel(hidden, s0, s1, s2, s3, far, out):
    mix = s0[...] + s1[...].astype(F32) + s2[...].astype(F32) + s3[...].astype(F32) + far[...].astype(F32)
    out[...] = (hidden[...].astype(F32) + mix).astype(BF)


def after(x, y):
    return lax.optimization_barrier((x, y))[0]


def swap_exp(x, mask):
    return lax.ppermute(x, "exp", [(i, i ^ mask) for i in range(16)])


def swap_ctx(x, mask):
    return lax.ppermute(x, "ctx", [(i, i ^ mask) for i in range(16)])


def turn_z(x, step):
    return lax.ppermute(x, "ctx", [(i, (i & 8) | ((i + step) & 7)) for i in range(16)])


def local(
    tokens,
    attn_gain,
    query_gain,
    key_gain,
    query_weight,
    key_weight,
    value_weight,
    out_weight,
    moe_gain,
    route_ids,
    route_weights,
    gate_weight,
    up_weight,
    down_weight,
):
    ctx = lax.axis_index("ctx").astype(jnp.int32)
    me = lax.axis_index("exp").astype(jnp.int32)
    y = (me >> 1) & 3
    info = jnp.stack([ctx, me, y, me >> 3, me & 1])
    planes = [list(range(8)), list(range(8, 16))]

    w_out = lax.all_gather(out_weight, "exp", axis=0, tiled=True, axis_index_groups=planes)
    [route] = call(route_kernel, (route_ids, route_weights), [((ROWS, 128), BF)], scalars=False)

    exponent = jnp.arange(HD // 2, dtype=F32) * (2.0 / HD)
    inverse = jnp.power(jnp.float32(ROPE_BASE), -exponent)
    owners = me ^ (2 * jnp.arange(4, dtype=jnp.int32))
    positions = (ctx * 1024 + owners[:, None] * ROWS + jnp.arange(ROWS, dtype=jnp.int32)[None, :]).reshape(-1)
    angles = positions.astype(F32)[:, None] * inverse[None, :]
    cosine, sine = jnp.cos(angles), jnp.sin(angles)
    cosine = jnp.concatenate([cosine, cosine], axis=1)
    sine = jnp.concatenate([-sine, sine], axis=1)

    w_far = swap_exp(query_weight, 8)
    w_core = swap_exp(query_weight, 1)
    [normed] = call(norm_kernel, (tokens, attn_gain[None]), [((ROWS, D), BF)], scalars=False, moved=MB)
    near = [swap_exp(normed, 2 * i) for i in (1, 2, 3)]
    own, other = call(
        kv_kernel,
        (info, normed, key_weight, value_weight, key_gain[None], cosine, sine),
        [((ROWS, 2 * HD), BF)] * 2,
        flops=ROWS * D * 1024,
        moved=2 * MB,
        in_hbm=(2, 3),
        scratch=[pltpu.VMEM((D, 2 * HD), BF), pltpu.VMEM((D, 2 * HD), BF), pltpu.SemaphoreType.DMA((2,))],
    )
    other = swap_exp(other, 8)
    w_far = after(w_far, (near, other))
    w_far_core = swap_exp(w_far, 1)
    pair = jnp.concatenate([own, other], axis=0)
    pair_in = swap_ctx(pair, 8)
    pair = jnp.stack([pair, pair_in])
    quad = jnp.stack([pair, turn_z(pair, 4)])
    below, above = turn_z(quad, 1), turn_z(quad, -1)
    keys = [quad, below, above, turn_z(below[:1], 1), turn_z(above[:1], -1)]

    mine, far = call(
        query_kernel,
        (info, normed, *near, query_weight, w_core, w_far, w_far_core, query_gain[None], cosine, sine),
        [((2, 256, HD), BF)] * 2,
        flops=256 * D * 1024,
        moved=4 * MB,
        scratch=[pltpu.VMEM((256, D), BF)],
    )
    far = swap_exp(after(far, pair_in), 8)
    both = jnp.stack([mine, after(far, quad)])
    queries = jnp.stack([both] + [swap_exp(both, 2 * i) for i in (1, 2, 3)])
    queries_core = swap_exp(after(queries, (below, above)), 1)

    def attend(which, q):
        return call(
            functools.partial(attend_kernel, which),
            (info, q, *keys),
            [((4, ROWS, WIDE), BF)],
            flops=2048 * 2048 * 512,
            moved=3 * MB,
            scratch=[
                pltpu.VMEM((2048, HD), BF),
                pltpu.VMEM((2048, 2 * HD), BF),
                pltpu.VMEM((512, 2 * HD), F32),
            ],
        )[0]

    def fold(part, part_core):
        parts = call(
            fold_kernel, (info, part, swap_exp(part_core, 1)), [((ROWS, WIDE), BF)] * 4, moved=2 * MB
        )
        return [parts[0]] + [swap_exp(parts[i], 2 * i) for i in (1, 2, 3)]

    a_far = attend(8, queries)
    a_far_core = attend(9, after(queries_core, a_far))
    a_near_core = attend(1, after(queries_core, a_far_core))
    a_near = attend(0, after(queries, (a_near_core, w_out)))
    sums_far, sums_near = fold(a_far, a_far_core), fold(a_near, a_near_core)
    part_in = swap_exp(project(after(sums_far, sums_near[0]), w_out, BF), 8)
    part = project(sums_near, w_out, F32)
    hidden, moe_in = call(
        hidden_kernel,
        (tokens, part, part_in, moe_gain[None], route),
        [((ROWS, D), BF), ((ROWS, D + 128), BF)],
        scalars=False,
        moved=2 * MB,
    )

    moe_far = swap_exp(moe_in, 8)
    m_near = [moe_in] + [swap_exp(moe_in, 2 * i) for i in (1, 2, 3)]
    moe_far = after(moe_far, (m_near[1], m_near[3]))
    m_far = jnp.stack([moe_far] + [swap_exp(moe_far, 2 * i) for i in (1, 2, 3)])
    m_near = jnp.stack(m_near)
    m_near_core, m_far_core = swap_exp(m_near, 1), swap_exp(m_far, 1)

    def expert(rows):
        return call(
            expert_kernel,
            (info, rows, gate_weight, up_weight, down_weight),
            [((4, ROWS, D), BF)],
            flops=4 * ROWS * D * FF * 6,
            moved=12 * MB,
            limit=12,
            scratch=[pltpu.VMEM((4 * ROWS, FF), BF)],
        )[0]

    def run_expert(keep_in, swap_in):
        keep = expert(keep_in)
        swap = expert(after(swap_in, keep))
        swap_back = swap_exp(swap, 1)
        s = call(
            combine_kernel,
            (keep, swap_back),
            [((ROWS, D), F32)] + [((ROWS, D), BF)] * 3,
            scalars=False,
            moved=4 * MB,
        )
        return [s[0]] + [swap_exp(s[i], 2 * i) for i in (1, 2, 3)]

    s_near = run_expert(m_near, m_near_core)
    s_far = run_expert(m_far, m_far_core)
    [out_far] = call(total_kernel, tuple(s_far), [((ROWS, D), BF)], scalars=False, moved=2 * MB)
    [out] = call(
        final_kernel, (hidden, *s_near, swap_exp(out_far, 8)), [((ROWS, D), BF)], scalars=False, moved=2 * MB
    )
    return out


def solution(mesh):
    rows = P(("ctx", "exp"), None)
    return jax.shard_map(
        local,
        mesh=mesh,
        in_specs=(
            rows,
            P(),
            P(),
            P(),
            P(None, "exp"),
            P(),
            P(),
            P("exp", None),
            P(),
            rows,
            rows,
            P("exp", None, None),
            P("exp", None, None),
            P("exp", None, None),
        ),
        out_specs=rows,
        check_vma=False,
    )
```

```python
import functools

import jax
import jax.numpy as jnp
from jax import lax
from jax.experimental import pallas as pl
from jax.experimental.pallas import tpu as pltpu
from jax.sharding import PartitionSpec as P

EPS = 1e-06
ROPE_BASE = 1000000.0
HD = 128
D = 2048
FF = 768
ROWS = 64
WIDE = 8 * HD + 128
LOG2E = 1.4426950408889634
MB = 1 << 20
BF = jnp.bfloat16
F32 = jnp.float32

VM = pl.BlockSpec(memory_space=pltpu.VMEM)
SM = pl.BlockSpec(memory_space=pltpu.SMEM)
ANY = pl.BlockSpec(memory_space=pl.ANY)


def call(kernel, args, outs, flops=0, moved=0, scratch=(), scalars=True, limit=12, in_hbm=()):
    specs = [ANY if i in in_hbm else SM if scalars and i == 0 else VM for i in range(len(args))]
    return pl.pallas_call(
        kernel,
        out_shape=[jax.ShapeDtypeStruct(s, t) for s, t in outs],
        in_specs=specs,
        out_specs=[VM] * len(outs),
        scratch_shapes=list(scratch),
        compiler_params=pltpu.CompilerParams(vmem_limit_bytes=limit * MB),
        cost_estimate=pl.CostEstimate(flops=flops, bytes_accessed=moved, transcendentals=0),
    )(*args)


def rms(values, gain):
    factor = lax.rsqrt(jnp.mean(values * values, axis=-1, keepdims=True) + EPS)
    return values * factor * gain


def rope(values, cosine, sine):
    return values * cosine + pltpu.roll(values, HD // 2, 1) * sine


def norm_kernel(tokens, gain, out):
    out[...] = rms(tokens[...].astype(F32), gain[...]).astype(BF)


def kv_kernel(info, normed, key_weight, value_weight, gain, cosine, sine, own, other, kw, vw, sems):
    plane = info[3]
    loads = [pltpu.make_async_copy(key_weight, kw, sems.at[0]), pltpu.make_async_copy(value_weight, vw, sems.at[1])]
    for load in loads:
        load.start()
    x = normed[...]
    loads[0].wait()
    keys = jnp.dot(x, kw[...], preferred_element_type=F32)
    loads[1].wait()
    vals = jnp.dot(x, vw[...], preferred_element_type=F32).astype(BF)
    cos, sin = cosine[0:ROWS], sine[0:ROWS]
    k0 = rope(rms(keys[:, :HD], gain[...]), cos, sin)
    k1 = rope(rms(keys[:, HD:], gain[...]), cos, sin)
    v0, v1 = vals[:, :HD].astype(F32), vals[:, HD:].astype(F32)
    first = plane == 0
    own[:, :HD] = jnp.where(first, k0, k1).astype(BF)
    own[:, HD:] = jnp.where(first, v0, v1).astype(BF)
    other[:, :HD] = jnp.where(first, k1, k0).astype(BF)
    other[:, HD:] = jnp.where(first, v1, v0).astype(BF)


def query_kernel(info, r0, r1, r2, r3, f0, f1, f2, f3, w_own, w_core, gain, cosine, sine, out, x_s):
    core = info[4]
    for i, r in enumerate((r0, r1, r2, r3, f0, f1, f2, f3)):
        x_s[i * ROWS : (i + 1) * ROWS] = r[...]
    cos, sin = cosine[...], sine[...]
    scale = gain[...] * (LOG2E * HD**-0.5)
    q = jnp.dot(x_s[...], jnp.concatenate([w_own[...], w_core[...]], axis=1), preferred_element_type=F32)
    first = rope(rms(q[:, :HD], scale), cos, sin).astype(BF)
    second = rope(rms(q[:, HD:], scale), cos, sin).astype(BF)
    for plane in range(2):
        rows = slice(plane * 256, (plane + 1) * 256)
        out[plane, core] = first[rows]
        out[plane, 1 - core] = second[rows]


KEYS = 512


def attend_kernel(which, info, q, t0, t1, t2, t3, t4, out, k_s, v_s, acc):
    ctx, me = info[0], info[1]
    base = jnp.bitwise_xor(me, which)
    y = jnp.bitwise_and(jnp.right_shift(me, 1), 3)
    at = 0
    for t, distance in ((t0, (0, 4)), (t1, (-1, 3)), (t2, (1, 5)), (t3, (-2,)), (t4, (2,))):
        for j, d in enumerate(distance):
            for i in range(2):
                z = jnp.bitwise_and(ctx + (8 + d), 7)
                source = jnp.bitwise_and(jnp.bitwise_xor(ctx, 8 * i), 8) + z
                valid = source <= ctx
                k_s[at : at + 128] = t[j, i, :, :HD]
                v_s[at : at + 128, :HD] = jnp.where(valid, t[j, i, :, HD:].astype(F32), 0.0).astype(BF)
                v_s[at : at + 128, HD:] = jnp.full((128, HD), jnp.where(valid, 1.0, 0.0), F32).astype(BF)
                at += 128
    out[:, :, 8 * HD :] = jnp.zeros((4, ROWS, 128), BF)
    lane = lax.broadcasted_iota(jnp.int32, (ROWS, 128), 1)

    def per_piece(dd, carry):
        row = lax.broadcasted_iota(jnp.int32, (256, 1), 0)
        key = lax.broadcasted_iota(jnp.int32, (256, 128), 1)
        key_dev = jnp.bitwise_xor(me, jnp.bitwise_and(jnp.right_shift(key, 6), 1) * 8)
        row_dev = jnp.bitwise_xor(base, jnp.bitwise_xor(jnp.right_shift(row, 6), dd) * 2)
        allowed = key_dev * ROWS + jnp.bitwise_and(key, 63) <= row_dev * ROWS + jnp.bitwise_and(row, 63)
        for p in range(2):
            qv = q[dd, which >> 3, p]
            total = None
            for c in range(0, 2048, KEYS):
                s = lax.dot_general(
                    qv, k_s[c : c + KEYS], (((1,), (1,)), ((), ())), preferred_element_type=F32
                )
                w = jnp.exp2(s)
                if c == 0:
                    w = jnp.concatenate([jnp.where(allowed, w[:, :128], 0.0), w[:, 128:]], axis=1)
                o = jnp.dot(w.astype(BF), v_s[c : c + KEYS], preferred_element_type=F32)
                total = o if total is None else total + o
            acc[p * 256 : (p + 1) * 256] = total
        for p in range(2):
            head = jnp.bitwise_xor(y, dd) * 2 + p
            for i in range(4):
                rows = jnp.bitwise_xor(jnp.bitwise_xor(y, dd), i)
                block = acc[p * 256 + i * ROWS : p * 256 + (i + 1) * ROWS]
                out[rows, :, pl.ds(pl.multiple_of(head * HD, HD), HD)] = block[:, :HD].astype(BF)
                den = block[:, HD:]
                high = den.astype(BF).astype(F32)
                old = out[rows, :, 8 * HD :].astype(F32)
                new = jnp.where(lane == head, high, jnp.where(lane == head + 8, den - high, old))
                out[rows, :, 8 * HD :] = new.astype(BF)
        return carry

    lax.fori_loop(0, 4, per_piece, 0, unroll=True)


def fold_kernel(info, part, part_in, s0, s1, s2, s3):
    y = info[2]
    for i, s in enumerate((s0, s1, s2, s3)):
        at = jnp.bitwise_xor(y, i)
        s[...] = (part[at].astype(F32) + part_in[at].astype(F32)).astype(BF)


def project_kernel(s0, s1, s2, s3, weight, out, x_s, w_s, sems):
    cols = [slice(n * 512, (n + 1) * 512) for n in range(4)]
    loads = [pltpu.make_async_copy(weight.at[:, c], w_s.at[:, c], sems.at[n]) for n, c in enumerate(cols)]
    for load in loads:
        load.start()
    total = s0[...].astype(F32) + s1[...].astype(F32) + s2[...].astype(F32) + s3[...].astype(F32)
    for h in range(8):
        den = total[:, 8 * HD + h : 8 * HD + h + 1] + total[:, 8 * HD + 8 + h : 8 * HD + 9 + h]
        x_s[:, h * HD : (h + 1) * HD] = (total[:, h * HD : (h + 1) * HD] / den).astype(BF)
    x = x_s[...]
    for c, load in zip(cols, loads):
        load.wait()
        out[:, c] = jnp.dot(x, w_s[:, c], preferred_element_type=F32).astype(out.dtype)


def project(parts, weight, kind):
    return call(
        project_kernel,
        (*parts, weight),
        [((ROWS, D), kind)],
        scalars=False,
        in_hbm=(4,),
        flops=ROWS * 2048 * 2048,
        moved=5 * MB,
        limit=50,
        scratch=[pltpu.VMEM((ROWS, 8 * HD), BF), pltpu.VMEM((8 * HD, D), BF), pltpu.SemaphoreType.DMA((4,))],
    )[0]


def route_kernel(ids, weights, out):
    lane = lax.broadcasted_iota(jnp.int32, (ROWS, 128), 1)
    table = jnp.zeros((ROWS, 128), F32)
    for k in range(8):
        expert, weight = ids[:, k : k + 1], weights[:, k : k + 1]
        high = weight.astype(BF).astype(F32)
        table = jnp.where(lane == expert, high, jnp.where(lane == expert + 16, weight - high, table))
    out[...] = table.astype(BF)


def hidden_kernel(tokens, part, part_in, gain, route, hidden, moe_in):
    h = (tokens[...].astype(F32) + (part[...] + part_in[...].astype(F32))).astype(BF)
    hidden[...] = h
    moe_in[:, :D] = rms(h.astype(F32), gain[...]).astype(BF)
    moe_in[:, D:] = route[...]


def expert_kernel(info, rows, gate, up, down, out, inner_s):
    me = info[1]
    lane = lax.broadcasted_iota(jnp.int32, (4 * ROWS, 128), 1)
    both = rows[...].reshape(4 * ROWS, D + 128)
    x = both[:, :D]
    w = jnp.where((lane == me) | (lane == me + 16), both[:, D:].astype(F32), 0.0)
    w = jnp.broadcast_to(jnp.sum(w, axis=1, keepdims=True), (4 * ROWS, 256))
    for n in range(FF // 256):
        c = slice(n * 256, (n + 1) * 256)
        g = jnp.dot(x, gate[0, :, c], preferred_element_type=F32)
        u = jnp.dot(x, up[0, :, c], preferred_element_type=F32)
        inner_s[:, c] = (g / (1.0 + jnp.exp(-g)) * u).astype(BF)
    inner = inner_s[...]
    for n in range(D // 256):
        c = slice(n * 256, (n + 1) * 256)
        res = jnp.dot(inner, down[0, :, c], preferred_element_type=F32).astype(BF).astype(F32)
        out[:, :, c] = (w * res).astype(BF).reshape(4, ROWS, 256)


def combine_kernel(keep, swap_in, s0, s1, s2, s3):
    for i, s in enumerate((s0, s1, s2, s3)):
        s[...] = (keep[i].astype(F32) + swap_in[i].astype(F32)).astype(s.dtype)


def total_kernel(s0, s1, s2, s3, out):
    out[...] = (s0[...] + s1[...].astype(F32) + s2[...].astype(F32) + s3[...].astype(F32)).astype(BF)


def final_kernel(hidden, s0, s1, s2, s3, far, out):
    mix = s0[...] + s1[...].astype(F32) + s2[...].astype(F32) + s3[...].astype(F32) + far[...].astype(F32)
    out[...] = (hidden[...].astype(F32) + mix).astype(BF)


def after(x, y):
    return lax.optimization_barrier((x, y))[0]


def swap_exp(x, mask):
    return lax.ppermute(x, "exp", [(i, i ^ mask) for i in range(16)])


def swap_ctx(x, mask):
    return lax.ppermute(x, "ctx", [(i, i ^ mask) for i in range(16)])


def turn_z(x, step):
    return lax.ppermute(x, "ctx", [(i, (i & 8) | ((i + step) & 7)) for i in range(16)])


def local(
    tokens,
    attn_gain,
    query_gain,
    key_gain,
    query_weight,
    key_weight,
    value_weight,
    out_weight,
    moe_gain,
    route_ids,
    route_weights,
    gate_weight,
    up_weight,
    down_weight,
):
    ctx = lax.axis_index("ctx").astype(jnp.int32)
    me = lax.axis_index("exp").astype(jnp.int32)
    y = (me >> 1) & 3
    info = jnp.stack([ctx, me, y, me >> 3, me & 1])
    [route] = call(route_kernel, (route_ids, route_weights), [((ROWS, 128), BF)], scalars=False)

    exponent = jnp.arange(HD // 2, dtype=F32) * (2.0 / HD)
    inverse = jnp.power(jnp.float32(ROPE_BASE), -exponent)
    owners = me ^ (2 * jnp.arange(8, dtype=jnp.int32))
    positions = (ctx * 1024 + owners[:, None] * ROWS + jnp.arange(ROWS, dtype=jnp.int32)[None, :]).reshape(-1)
    angles = positions.astype(F32)[:, None] * inverse[None, :]
    cosine, sine = jnp.cos(angles), jnp.sin(angles)
    cosine = jnp.concatenate([cosine, cosine], axis=1)
    sine = jnp.concatenate([-sine, sine], axis=1)

    w_core = swap_exp(query_weight, 1)
    [normed] = call(norm_kernel, (tokens, attn_gain[None]), [((ROWS, D), BF)], scalars=False, moved=MB)
    rows_far = swap_exp(normed, 8)
    near = [swap_exp(normed, 2 * i) for i in (1, 2, 3)]
    own, other = call(
        kv_kernel,
        (info, after(normed, (near[0], near[2], rows_far)), key_weight, value_weight, key_gain[None], cosine, sine),
        [((ROWS, 2 * HD), BF)] * 2,
        flops=ROWS * D * 1024,
        moved=2 * MB,
        in_hbm=(2, 3),
        scratch=[pltpu.VMEM((D, 2 * HD), BF), pltpu.VMEM((D, 2 * HD), BF), pltpu.SemaphoreType.DMA((2,))],
    )
    far = [swap_exp(rows_far, 2 * i) for i in (1, 2, 3)]
    other = swap_exp(after(other, near[1]), 8)
    pair = jnp.concatenate([own, other], axis=0)
    pair_in = swap_ctx(pair, 8)
    pair = jnp.stack([pair, pair_in])
    quad = jnp.stack([pair, turn_z(after(pair, (far[0], far[2])), 4)])
    below, above = turn_z(quad, 1), turn_z(quad, -1)
    keys = [quad, below, above, turn_z(below[:1], 1), turn_z(above[:1], -1)]

    [both] = call(
        query_kernel,
        (
            info,
            normed,
            *near,
            rows_far,
            *far,
            query_weight,
            after(w_core, pair_in),
            query_gain[None],
            cosine,
            sine,
        ),
        [((2, 2, 256, HD), BF)],
        flops=512 * D * 512,
        moved=4 * MB,
        scratch=[pltpu.VMEM((512, D), BF)],
    )
    both = after(both, quad)
    parts = [swap_exp(both, 2 * i) for i in (1, 2, 3)]
    queries = jnp.stack([both] + after(parts, (below, above)))
    queries_core = swap_exp(queries, 1)
    planes = [list(range(8)), list(range(8, 16))]
    w_out = lax.all_gather(after(out_weight, queries), "exp", axis=0, tiled=True, axis_index_groups=planes)

    def attend(which, q):
        return call(
            functools.partial(attend_kernel, which),
            (info, q, *keys),
            [((4, ROWS, WIDE), BF)],
            flops=2048 * 2048 * 512,
            moved=3 * MB,
            scratch=[
                pltpu.VMEM((2048, HD), BF),
                pltpu.VMEM((2048, 2 * HD), BF),
                pltpu.VMEM((512, 2 * HD), F32),
            ],
        )[0]

    def fold(part, part_core):
        parts = call(
            fold_kernel, (info, part, swap_exp(part_core, 1)), [((ROWS, WIDE), BF)] * 4, moved=2 * MB
        )
        return [parts[0]] + [swap_exp(parts[i], 2 * i) for i in (1, 2, 3)]

    a_far = attend(8, queries)
    a_far_core = attend(9, after(queries_core, a_far))
    a_near_core = attend(1, after(queries_core, a_far_core))
    a_near = attend(0, after(queries, a_near_core))
    sums_far, sums_near = fold(a_far, a_far_core), fold(a_near, a_near_core)
    part_in = swap_exp(project(after(sums_far, sums_near[0]), w_out, BF), 8)
    part = project(sums_near, w_out, F32)
    hidden, moe_in = call(
        hidden_kernel,
        (tokens, part, part_in, moe_gain[None], route),
        [((ROWS, D), BF), ((ROWS, D + 128), BF)],
        scalars=False,
        moved=2 * MB,
    )

    moe_far = swap_exp(moe_in, 8)
    near_1, near_3 = swap_exp(moe_in, 2), swap_exp(moe_in, 6)
    moe_far = after(moe_far, (near_1, near_3))
    far_1, far_2, far_3 = [swap_exp(moe_far, 2 * i) for i in (1, 2, 3)]
    near_2 = swap_exp(after(moe_in, (far_1, far_3)), 4)
    m_far = jnp.stack([moe_far, far_1, far_2, far_3])
    m_near = jnp.stack([moe_in, near_1, near_2, near_3])
    m_near_core, m_far_core = swap_exp(m_near, 1), swap_exp(m_far, 1)

    def expert(rows):
        return call(
            expert_kernel,
            (info, rows, gate_weight, up_weight, down_weight),
            [((4, ROWS, D), BF)],
            flops=4 * ROWS * D * FF * 6,
            moved=12 * MB,
            limit=12,
            scratch=[pltpu.VMEM((4 * ROWS, FF), BF)],
        )[0]

    def run_expert(keep_in, swap_in):
        keep = expert(keep_in)
        swap = expert(after(swap_in, keep))
        return call(
            combine_kernel,
            (keep, swap_exp(swap, 1)),
            [((ROWS, D), F32)] + [((ROWS, D), BF)] * 3,
            scalars=False,
            moved=4 * MB,
        )

    s_far = run_expert(m_far, m_far_core)
    s_near = run_expert(m_near, m_near_core)
    s_far = [s_far[0]] + [swap_exp(s_far[i], 2 * i) for i in (1, 2, 3)]
    s_near = [s_near[0]] + [swap_exp(s_near[i], 2 * i) for i in (1, 2, 3)]
    [out_far] = call(total_kernel, tuple(s_far), [((ROWS, D), BF)], scalars=False, moved=2 * MB)
    [out] = call(
        final_kernel, (hidden, *s_near, swap_exp(out_far, 8)), [((ROWS, D), BF)], scalars=False, moved=2 * MB
    )
    return out


def solution(mesh):
    rows = P(("ctx", "exp"), None)
    return jax.shard_map(
        local,
        mesh=mesh,
        in_specs=(
            rows,
            P(),
            P(),
            P(),
            P(None, "exp"),
            P(),
            P(),
            P("exp", None),
            P(),
            rows,
            rows,
            P("exp", None, None),
            P("exp", None, None),
            P("exp", None, None),
        ),
        out_specs=rows,
        check_vma=False,
    )
```

```python
import functools

import jax
import jax.numpy as jnp
from jax import lax
from jax.experimental import pallas as pl
from jax.experimental.pallas import tpu as pltpu
from jax.sharding import PartitionSpec as P

EPS = 1e-06
ROPE_BASE = 1000000.0
HD = 128
D = 2048
FF = 768
ROWS = 64
WIDE = 8 * HD + 128
LOG2E = 1.4426950408889634
MB = 1 << 20
BF = jnp.bfloat16
F32 = jnp.float32

VM = pl.BlockSpec(memory_space=pltpu.VMEM)
SM = pl.BlockSpec(memory_space=pltpu.SMEM)
ANY = pl.BlockSpec(memory_space=pl.ANY)


def call(kernel, args, outs, flops=0, moved=0, scratch=(), scalars=True, limit=12, in_hbm=()):
    specs = [ANY if i in in_hbm else SM if scalars and i == 0 else VM for i in range(len(args))]
    return pl.pallas_call(
        kernel,
        out_shape=[jax.ShapeDtypeStruct(s, t) for s, t in outs],
        in_specs=specs,
        out_specs=[VM] * len(outs),
        scratch_shapes=list(scratch),
        compiler_params=pltpu.CompilerParams(vmem_limit_bytes=limit * MB),
        cost_estimate=pl.CostEstimate(flops=flops, bytes_accessed=moved, transcendentals=0),
    )(*args)


def rms(values, gain):
    factor = lax.rsqrt(jnp.mean(values * values, axis=-1, keepdims=True) + EPS)
    return values * factor * gain


def rope(values, cosine, sine):
    return values * cosine + pltpu.roll(values, HD // 2, 1) * sine


def norm_kernel(tokens, gain, out):
    out[...] = rms(tokens[...].astype(F32), gain[...]).astype(BF)


def kv_kernel(info, normed, key_weight, value_weight, gain, cosine, sine, own, other, kw, vw, sems):
    plane = info[3]
    loads = [pltpu.make_async_copy(key_weight, kw, sems.at[0]), pltpu.make_async_copy(value_weight, vw, sems.at[1])]
    for load in loads:
        load.start()
    x = normed[...]
    loads[0].wait()
    keys = jnp.dot(x, kw[...], preferred_element_type=F32)
    loads[1].wait()
    vals = jnp.dot(x, vw[...], preferred_element_type=F32).astype(BF)
    cos, sin = cosine[0:ROWS], sine[0:ROWS]
    k0 = rope(rms(keys[:, :HD], gain[...]), cos, sin)
    k1 = rope(rms(keys[:, HD:], gain[...]), cos, sin)
    v0, v1 = vals[:, :HD].astype(F32), vals[:, HD:].astype(F32)
    first = plane == 0
    own[:, :HD] = jnp.where(first, k0, k1).astype(BF)
    own[:, HD:] = jnp.where(first, v0, v1).astype(BF)
    other[:, :HD] = jnp.where(first, k1, k0).astype(BF)
    other[:, HD:] = jnp.where(first, v1, v0).astype(BF)


def query_kernel(info, r0, r1, r2, r3, w_own, w_core, w_far, w_far_core, gain, cosine, sine, mine, far, x_s):
    core = info[4]
    for i, r in enumerate((r0, r1, r2, r3)):
        x_s[i * ROWS : (i + 1) * ROWS] = r[...]
    x = x_s[...]
    cos, sin = cosine[...], sine[...]
    scale = gain[...] * (LOG2E * HD**-0.5)
    for out, first, second in ((far, w_far, w_far_core), (mine, w_own, w_core)):
        q = jnp.dot(x, jnp.concatenate([first[...], second[...]], axis=1), preferred_element_type=F32)
        out[core] = rope(rms(q[:, :HD], scale), cos, sin).astype(BF)
        out[1 - core] = rope(rms(q[:, HD:], scale), cos, sin).astype(BF)


KEYS = 512


def attend_kernel(which, info, q, t0, t1, t2, t3, t4, out, k_s, v_s, acc):
    ctx, me = info[0], info[1]
    base = jnp.bitwise_xor(me, which)
    y = jnp.bitwise_and(jnp.right_shift(me, 1), 3)
    at = 0
    for t, distance in ((t0, (0, 4)), (t1, (-1, 3)), (t2, (1, 5)), (t3, (-2,)), (t4, (2,))):
        for j, d in enumerate(distance):
            for i in range(2):
                z = jnp.bitwise_and(ctx + (8 + d), 7)
                source = jnp.bitwise_and(jnp.bitwise_xor(ctx, 8 * i), 8) + z
                valid = source <= ctx
                k_s[at : at + 128] = t[j, i, :, :HD]
                v_s[at : at + 128, :HD] = jnp.where(valid, t[j, i, :, HD:].astype(F32), 0.0).astype(BF)
                v_s[at : at + 128, HD:] = jnp.full((128, HD), jnp.where(valid, 1.0, 0.0), F32).astype(BF)
                at += 128
    out[:, :, 8 * HD :] = jnp.zeros((4, ROWS, 128), BF)
    lane = lax.broadcasted_iota(jnp.int32, (ROWS, 128), 1)

    def per_piece(dd, carry):
        row = lax.broadcasted_iota(jnp.int32, (256, 1), 0)
        key = lax.broadcasted_iota(jnp.int32, (256, 128), 1)
        key_dev = jnp.bitwise_xor(me, jnp.bitwise_and(jnp.right_shift(key, 6), 1) * 8)
        row_dev = jnp.bitwise_xor(base, jnp.bitwise_xor(jnp.right_shift(row, 6), dd) * 2)
        allowed = key_dev * ROWS + jnp.bitwise_and(key, 63) <= row_dev * ROWS + jnp.bitwise_and(row, 63)
        for p in range(2):
            qv = q[dd, which >> 3, p]
            total = None
            for c in range(0, 2048, KEYS):
                s = lax.dot_general(
                    qv, k_s[c : c + KEYS], (((1,), (1,)), ((), ())), preferred_element_type=F32
                )
                w = jnp.exp2(s)
                if c == 0:
                    w = jnp.concatenate([jnp.where(allowed, w[:, :128], 0.0), w[:, 128:]], axis=1)
                o = jnp.dot(w.astype(BF), v_s[c : c + KEYS], preferred_element_type=F32)
                total = o if total is None else total + o
            acc[p * 256 : (p + 1) * 256] = total
        for p in range(2):
            head = jnp.bitwise_xor(y, dd) * 2 + p
            for i in range(4):
                rows = jnp.bitwise_xor(jnp.bitwise_xor(y, dd), i)
                block = acc[p * 256 + i * ROWS : p * 256 + (i + 1) * ROWS]
                out[rows, :, pl.ds(pl.multiple_of(head * HD, HD), HD)] = block[:, :HD].astype(BF)
                den = block[:, HD:]
                high = den.astype(BF).astype(F32)
                old = out[rows, :, 8 * HD :].astype(F32)
                new = jnp.where(lane == head, high, jnp.where(lane == head + 8, den - high, old))
                out[rows, :, 8 * HD :] = new.astype(BF)
        return carry

    lax.fori_loop(0, 4, per_piece, 0, unroll=True)


def fold_kernel(info, part, part_in, s0, s1, s2, s3):
    y = info[2]
    for i, s in enumerate((s0, s1, s2, s3)):
        at = jnp.bitwise_xor(y, i)
        s[...] = (part[at].astype(F32) + part_in[at].astype(F32)).astype(BF)


def project_kernel(s0, s1, s2, s3, weight, out, x_s, w_s, sems):
    cols = [slice(n * 512, (n + 1) * 512) for n in range(4)]
    loads = [pltpu.make_async_copy(weight.at[:, c], w_s.at[:, c], sems.at[n]) for n, c in enumerate(cols)]
    for load in loads:
        load.start()
    total = s0[...].astype(F32) + s1[...].astype(F32) + s2[...].astype(F32) + s3[...].astype(F32)
    for h in range(8):
        den = total[:, 8 * HD + h : 8 * HD + h + 1] + total[:, 8 * HD + 8 + h : 8 * HD + 9 + h]
        x_s[:, h * HD : (h + 1) * HD] = (total[:, h * HD : (h + 1) * HD] / den).astype(BF)
    x = x_s[...]
    for c, load in zip(cols, loads):
        load.wait()
        out[:, c] = jnp.dot(x, w_s[:, c], preferred_element_type=F32).astype(out.dtype)


def project(parts, weight, kind):
    return call(
        project_kernel,
        (*parts, weight),
        [((ROWS, D), kind)],
        scalars=False,
        in_hbm=(4,),
        limit=50,
        flops=ROWS * 2048 * 2048,
        moved=5 * MB,
        scratch=[pltpu.VMEM((ROWS, 8 * HD), BF), pltpu.VMEM((8 * HD, D), BF), pltpu.SemaphoreType.DMA((4,))],
    )[0]


def route_kernel(ids, weights, out):
    lane = lax.broadcasted_iota(jnp.int32, (ROWS, 128), 1)
    table = jnp.zeros((ROWS, 128), F32)
    for k in range(8):
        expert, weight = ids[:, k : k + 1], weights[:, k : k + 1]
        high = weight.astype(BF).astype(F32)
        table = jnp.where(lane == expert, high, jnp.where(lane == expert + 16, weight - high, table))
    out[...] = table.astype(BF)


def hidden_kernel(tokens, part, part_in, gain, route, hidden, moe_in):
    h = (tokens[...].astype(F32) + (part[...] + part_in[...].astype(F32))).astype(BF)
    hidden[...] = h
    moe_in[:, :D] = rms(h.astype(F32), gain[...]).astype(BF)
    moe_in[:, D:] = route[...]


def expert_kernel(count, info, *refs):
    me = info[1]
    gate, up, down = refs[count : count + 3]
    inner_s = refs[-1]
    lane = lax.broadcasted_iota(jnp.int32, (4 * ROWS, 128), 1)
    for rows, out in zip(refs[:count], refs[count + 3 : -1]):
        both = rows[...].reshape(4 * ROWS, D + 128)
        x = both[:, :D]
        w = jnp.where((lane == me) | (lane == me + 16), both[:, D:].astype(F32), 0.0)
        w = jnp.broadcast_to(jnp.sum(w, axis=1, keepdims=True), (4 * ROWS, 256))
        for n in range(FF // 256):
            c = slice(n * 256, (n + 1) * 256)
            g = jnp.dot(x, gate[0, :, c], preferred_element_type=F32)
            u = jnp.dot(x, up[0, :, c], preferred_element_type=F32)
            inner_s[:, c] = (g / (1.0 + jnp.exp(-g)) * u).astype(BF)
        inner = inner_s[...]
        for n in range(D // 256):
            c = slice(n * 256, (n + 1) * 256)
            res = jnp.dot(inner, down[0, :, c], preferred_element_type=F32).astype(BF).astype(F32)
            out[:, :, c] = (w * res).astype(BF).reshape(4, ROWS, 256)


def combine_kernel(keep, swap_in, s0, s1, s2, s3):
    for i, s in enumerate((s0, s1, s2, s3)):
        s[...] = (keep[i].astype(F32) + swap_in[i].astype(F32)).astype(s.dtype)


def total_kernel(s0, s1, s2, s3, out):
    out[...] = (s0[...] + s1[...].astype(F32) + s2[...].astype(F32) + s3[...].astype(F32)).astype(BF)


def final_kernel(hidden, s0, s1, s2, s3, far, out):
    mix = s0[...] + s1[...].astype(F32) + s2[...].astype(F32) + s3[...].astype(F32) + far[...].astype(F32)
    out[...] = (hidden[...].astype(F32) + mix).astype(BF)


def after(x, y):
    return lax.optimization_barrier((x, y))[0]


def swap_exp(x, mask):
    return lax.ppermute(x, "exp", [(i, i ^ mask) for i in range(16)])


def swap_ctx(x, mask):
    return lax.ppermute(x, "ctx", [(i, i ^ mask) for i in range(16)])


def turn_z(x, step):
    return lax.ppermute(x, "ctx", [(i, (i & 8) | ((i + step) & 7)) for i in range(16)])


def local(
    tokens,
    attn_gain,
    query_gain,
    key_gain,
    query_weight,
    key_weight,
    value_weight,
    out_weight,
    moe_gain,
    route_ids,
    route_weights,
    gate_weight,
    up_weight,
    down_weight,
):
    ctx = lax.axis_index("ctx").astype(jnp.int32)
    me = lax.axis_index("exp").astype(jnp.int32)
    y = (me >> 1) & 3
    info = jnp.stack([ctx, me, y, me >> 3, me & 1])
    [route] = call(route_kernel, (route_ids, route_weights), [((ROWS, 128), BF)], scalars=False)

    exponent = jnp.arange(HD // 2, dtype=F32) * (2.0 / HD)
    inverse = jnp.power(jnp.float32(ROPE_BASE), -exponent)
    owners = me ^ (2 * jnp.arange(4, dtype=jnp.int32))
    positions = (ctx * 1024 + owners[:, None] * ROWS + jnp.arange(ROWS, dtype=jnp.int32)[None, :]).reshape(-1)
    angles = positions.astype(F32)[:, None] * inverse[None, :]
    cosine, sine = jnp.cos(angles), jnp.sin(angles)
    cosine = jnp.concatenate([cosine, cosine], axis=1)
    sine = jnp.concatenate([-sine, sine], axis=1)

    w_far = swap_exp(query_weight, 8)
    w_core = swap_exp(query_weight, 1)
    [normed] = call(norm_kernel, (tokens, attn_gain[None]), [((ROWS, D), BF)], scalars=False, moved=MB)
    near = [swap_exp(normed, 2 * i) for i in (1, 2, 3)]
    own, other = call(
        kv_kernel,
        (info, normed, key_weight, value_weight, key_gain[None], cosine, sine),
        [((ROWS, 2 * HD), BF)] * 2,
        flops=ROWS * D * 1024,
        moved=2 * MB,
        in_hbm=(2, 3),
        scratch=[pltpu.VMEM((D, 2 * HD), BF), pltpu.VMEM((D, 2 * HD), BF), pltpu.SemaphoreType.DMA((2,))],
    )
    other = swap_exp(other, 8)
    w_far = after(w_far, (near, other))
    w_far_core = swap_exp(w_far, 1)
    pair = jnp.concatenate([own, other], axis=0)
    pair_in = swap_ctx(pair, 8)
    pair = jnp.stack([pair, pair_in])
    quad = jnp.stack([pair, turn_z(pair, 4)])
    below, above = turn_z(quad, 1), turn_z(quad, -1)
    keys = [quad, below, above, turn_z(below[:1], 1), turn_z(above[:1], -1)]

    mine, far = call(
        query_kernel,
        (info, normed, *near, query_weight, w_core, w_far, w_far_core, query_gain[None], cosine, sine),
        [((2, 256, HD), BF)] * 2,
        flops=256 * D * 1024,
        moved=4 * MB,
        scratch=[pltpu.VMEM((256, D), BF)],
    )
    far = swap_exp(after(far, pair_in), 8)
    both = jnp.stack([mine, after(far, quad)])
    parts = [swap_exp(both, 2 * i) for i in (1, 2, 3)]
    queries = jnp.stack([both] + after(parts, (below, above)))
    queries_core = swap_exp(queries, 1)
    planes = [list(range(8)), list(range(8, 16))]
    w_out = lax.all_gather(after(out_weight, queries), "exp", axis=0, tiled=True, axis_index_groups=planes)

    def attend(which, q):
        return call(
            functools.partial(attend_kernel, which),
            (info, q, *keys),
            [((4, ROWS, WIDE), BF)],
            flops=2048 * 2048 * 512,
            moved=3 * MB,
            scratch=[
                pltpu.VMEM((2048, HD), BF),
                pltpu.VMEM((2048, 2 * HD), BF),
                pltpu.VMEM((512, 2 * HD), F32),
            ],
        )[0]

    def fold(part, part_core):
        parts = call(
            fold_kernel, (info, part, swap_exp(part_core, 1)), [((ROWS, WIDE), BF)] * 4, moved=2 * MB
        )
        return [parts[0]] + [swap_exp(parts[i], 2 * i) for i in (1, 2, 3)]

    a_far = attend(8, queries)
    a_far_core = attend(9, after(queries_core, a_far))
    a_near_core = attend(1, after(queries_core, a_far_core))
    a_near = attend(0, after(queries, a_near_core))
    sums_far, sums_near = fold(a_far, a_far_core), fold(a_near, a_near_core)
    part_in = swap_exp(project(after(sums_far, sums_near[0]), w_out, BF), 8)
    part = project(sums_near, w_out, F32)
    hidden, moe_in = call(
        hidden_kernel,
        (tokens, part, part_in, moe_gain[None], route),
        [((ROWS, D), BF), ((ROWS, D + 128), BF)],
        scalars=False,
        moved=2 * MB,
    )

    moe_far = swap_exp(moe_in, 8)
    near_1, near_2, near_3 = [swap_exp(moe_in, 2 * i) for i in (1, 2, 3)]
    m_near = jnp.stack(after([moe_in, near_1, near_2, near_3], moe_far))
    moe_far = after(moe_far, (near_1, near_3))
    far_1, far_3 = swap_exp(moe_far, 2), swap_exp(moe_far, 6)
    far_2 = swap_exp(after(moe_far, near_2), 4)

    def expert(*rows):
        return call(
            functools.partial(expert_kernel, len(rows)),
            (info, *rows, gate_weight, up_weight, down_weight),
            [((4, ROWS, D), BF)] * len(rows),
            flops=4 * ROWS * D * FF * 6 * len(rows),
            moved=12 * MB,
            limit=12,
            scratch=[pltpu.VMEM((4 * ROWS, FF), BF)],
        )

    def combine(keep, swap_in):
        s = call(
            combine_kernel,
            (keep, swap_in),
            [((ROWS, D), F32)] + [((ROWS, D), BF)] * 3,
            scalars=False,
            moved=4 * MB,
        )
        return [s[0]] + [swap_exp(s[i], 2 * i) for i in (1, 2, 3)]

    keep_near, swap_near = expert(m_near, swap_exp(m_near, 1))
    swap_near = swap_exp(after(swap_near, (far_1, far_3)), 1)
    m_far = jnp.stack(after([moe_far, far_1, far_2, far_3], keep_near))
    m_far_core = swap_exp(m_far, 1)
    [keep_far] = expert(m_far)
    [swap_far] = expert(after(m_far_core, keep_far))
    s_far = combine(keep_far, swap_exp(swap_far, 1))
    s_near = combine(keep_near, swap_near)
    [out_far] = call(total_kernel, tuple(s_far), [((ROWS, D), BF)], scalars=False, moved=2 * MB)
    [out] = call(
        final_kernel, (hidden, *s_near, swap_exp(out_far, 8)), [((ROWS, D), BF)], scalars=False, moved=2 * MB
    )
    return out


def solution(mesh):
    rows = P(("ctx", "exp"), None)
    return jax.shard_map(
        local,
        mesh=mesh,
        in_specs=(
            rows,
            P(),
            P(),
            P(),
            P(None, "exp"),
            P(),
            P(),
            P("exp", None),
            P(),
            rows,
            rows,
            P("exp", None, None),
            P("exp", None, None),
            P("exp", None, None),
        ),
        out_specs=rows,
        check_vma=False,
    )
```

```python
import functools

import jax
import jax.numpy as jnp
from jax import lax
from jax.experimental import pallas as pl
from jax.experimental.pallas import tpu as pltpu
from jax.sharding import PartitionSpec as P

EPS = 1e-06
ROPE_BASE = 1000000.0
HD = 128
D = 2048
FF = 768
ROWS = 64
WIDE = 8 * HD + 128
LOG2E = 1.4426950408889634
MB = 1 << 20
BF = jnp.bfloat16
F32 = jnp.float32

VM = pl.BlockSpec(memory_space=pltpu.VMEM)
SM = pl.BlockSpec(memory_space=pltpu.SMEM)
ANY = pl.BlockSpec(memory_space=pl.ANY)


def call(kernel, args, outs, flops=0, moved=0, scratch=(), scalars=True, limit=12, in_hbm=()):
    specs = [ANY if i in in_hbm else SM if scalars and i == 0 else VM for i in range(len(args))]
    return pl.pallas_call(
        kernel,
        out_shape=[jax.ShapeDtypeStruct(s, t) for s, t in outs],
        in_specs=specs,
        out_specs=[VM] * len(outs),
        scratch_shapes=list(scratch),
        compiler_params=pltpu.CompilerParams(vmem_limit_bytes=limit * MB),
        cost_estimate=pl.CostEstimate(flops=flops, bytes_accessed=moved, transcendentals=0),
    )(*args)


def rms(values, gain):
    factor = lax.rsqrt(jnp.mean(values * values, axis=-1, keepdims=True) + EPS)
    return values * factor * gain


def rope(values, cosine, sine):
    return values * cosine + pltpu.roll(values, HD // 2, 1) * sine


def norm_kernel(tokens, gain, out):
    out[...] = rms(tokens[...].astype(F32), gain[...]).astype(BF)


def kv_kernel(info, normed, key_weight, value_weight, gain, cosine, sine, own, other, kw, vw, sems):
    plane = info[3]
    loads = [pltpu.make_async_copy(key_weight, kw, sems.at[0]), pltpu.make_async_copy(value_weight, vw, sems.at[1])]
    for load in loads:
        load.start()
    x = normed[...]
    loads[0].wait()
    keys = jnp.dot(x, kw[...], preferred_element_type=F32)
    loads[1].wait()
    vals = jnp.dot(x, vw[...], preferred_element_type=F32).astype(BF)
    cos, sin = cosine[0:ROWS], sine[0:ROWS]
    k0 = rope(rms(keys[:, :HD], gain[...]), cos, sin)
    k1 = rope(rms(keys[:, HD:], gain[...]), cos, sin)
    v0, v1 = vals[:, :HD].astype(F32), vals[:, HD:].astype(F32)
    first = plane == 0
    own[:, :HD] = jnp.where(first, k0, k1).astype(BF)
    own[:, HD:] = jnp.where(first, v0, v1).astype(BF)
    other[:, :HD] = jnp.where(first, k1, k0).astype(BF)
    other[:, HD:] = jnp.where(first, v1, v0).astype(BF)


def query_kernel(info, r0, r1, r2, r3, w_own, w_core, w_far, w_far_core, gain, cosine, sine, mine, far, x_s):
    core = info[4]
    for i, r in enumerate((r0, r1, r2, r3)):
        x_s[i * ROWS : (i + 1) * ROWS] = r[...]
    x = x_s[...]
    cos, sin = cosine[...], sine[...]
    scale = gain[...] * (LOG2E * HD**-0.5)
    for out, first, second in ((far, w_far, w_far_core), (mine, w_own, w_core)):
        q = jnp.dot(x, jnp.concatenate([first[...], second[...]], axis=1), preferred_element_type=F32)
        out[core] = rope(rms(q[:, :HD], scale), cos, sin).astype(BF)
        out[1 - core] = rope(rms(q[:, HD:], scale), cos, sin).astype(BF)


KEYS = 512


def attend_kernel(which, info, q, t0, t1, t2, t3, t4, out, k_s, v_s, acc):
    ctx, me = info[0], info[1]
    base = jnp.bitwise_xor(me, which)
    y = jnp.bitwise_and(jnp.right_shift(me, 1), 3)
    at = 0
    for t, distance in ((t0, (0, 4)), (t1, (-1, 3)), (t2, (1, 5)), (t3, (-2,)), (t4, (2,))):
        for j, d in enumerate(distance):
            for i in range(2):
                z = jnp.bitwise_and(ctx + (8 + d), 7)
                source = jnp.bitwise_and(jnp.bitwise_xor(ctx, 8 * i), 8) + z
                valid = source <= ctx
                k_s[at : at + 128] = t[j, i, :, :HD]
                v_s[at : at + 128, :HD] = jnp.where(valid, t[j, i, :, HD:].astype(F32), 0.0).astype(BF)
                v_s[at : at + 128, HD:] = jnp.full((128, HD), jnp.where(valid, 1.0, 0.0), F32).astype(BF)
                at += 128
    out[:, :, 8 * HD :] = jnp.zeros((4, ROWS, 128), BF)
    lane = lax.broadcasted_iota(jnp.int32, (ROWS, 128), 1)

    def per_piece(dd, carry):
        row = lax.broadcasted_iota(jnp.int32, (256, 1), 0)
        key = lax.broadcasted_iota(jnp.int32, (256, 128), 1)
        key_dev = jnp.bitwise_xor(me, jnp.bitwise_and(jnp.right_shift(key, 6), 1) * 8)
        row_dev = jnp.bitwise_xor(base, jnp.bitwise_xor(jnp.right_shift(row, 6), dd) * 2)
        allowed = key_dev * ROWS + jnp.bitwise_and(key, 63) <= row_dev * ROWS + jnp.bitwise_and(row, 63)
        for p in range(2):
            qv = q[dd, which >> 3, p]
            total = None
            for c in range(0, 2048, KEYS):
                s = lax.dot_general(
                    qv, k_s[c : c + KEYS], (((1,), (1,)), ((), ())), preferred_element_type=F32
                )
                w = jnp.exp2(s)
                if c == 0:
                    w = jnp.concatenate([jnp.where(allowed, w[:, :128], 0.0), w[:, 128:]], axis=1)
                o = jnp.dot(w.astype(BF), v_s[c : c + KEYS], preferred_element_type=F32)
                total = o if total is None else total + o
            acc[p * 256 : (p + 1) * 256] = total
        for p in range(2):
            head = jnp.bitwise_xor(y, dd) * 2 + p
            for i in range(4):
                rows = jnp.bitwise_xor(jnp.bitwise_xor(y, dd), i)
                block = acc[p * 256 + i * ROWS : p * 256 + (i + 1) * ROWS]
                out[rows, :, pl.ds(pl.multiple_of(head * HD, HD), HD)] = block[:, :HD].astype(BF)
                den = block[:, HD:]
                high = den.astype(BF).astype(F32)
                old = out[rows, :, 8 * HD :].astype(F32)
                new = jnp.where(lane == head, high, jnp.where(lane == head + 8, den - high, old))
                out[rows, :, 8 * HD :] = new.astype(BF)
        return carry

    lax.fori_loop(0, 4, per_piece, 0, unroll=True)


def fold_kernel(info, part, part_in, s0, s1, s2, s3):
    y = info[2]
    for i, s in enumerate((s0, s1, s2, s3)):
        at = jnp.bitwise_xor(y, i)
        s[...] = (part[at].astype(F32) + part_in[at].astype(F32)).astype(BF)


def project_kernel(s0, s1, s2, s3, weight, out, x_s):
    total = s0[...].astype(F32) + s1[...].astype(F32) + s2[...].astype(F32) + s3[...].astype(F32)
    for h in range(8):
        den = total[:, 8 * HD + h : 8 * HD + h + 1] + total[:, 8 * HD + 8 + h : 8 * HD + 9 + h]
        x_s[:, h * HD : (h + 1) * HD] = (total[:, h * HD : (h + 1) * HD] / den).astype(BF)
    x = x_s[...]
    for n in range(4):
        c = slice(n * 512, (n + 1) * 512)
        out[:, c] = jnp.dot(x, weight[:, c], preferred_element_type=F32).astype(out.dtype)


def project(parts, weight, kind):
    return call(
        project_kernel,
        (*parts, weight),
        [((ROWS, D), kind)],
        scalars=False,
        flops=ROWS * 2048 * 2048,
        moved=5 * MB,
        scratch=[pltpu.VMEM((ROWS, 8 * HD), BF)],
    )[0]


def route_kernel(ids, weights, out):
    lane = lax.broadcasted_iota(jnp.int32, (ROWS, 128), 1)
    table = jnp.zeros((ROWS, 128), F32)
    for k in range(8):
        expert, weight = ids[:, k : k + 1], weights[:, k : k + 1]
        high = weight.astype(BF).astype(F32)
        table = jnp.where(lane == expert, high, jnp.where(lane == expert + 16, weight - high, table))
    out[...] = table.astype(BF)


def hidden_kernel(tokens, part, part_in, gain, route, hidden, moe_in):
    h = (tokens[...].astype(F32) + (part[...] + part_in[...].astype(F32))).astype(BF)
    hidden[...] = h
    moe_in[:, :D] = rms(h.astype(F32), gain[...]).astype(BF)
    moe_in[:, D:] = route[...]


def expert_kernel(count, info, *refs):
    me = info[1]
    gate, up, down = refs[count : count + 3]
    inner_s = refs[-1]
    lane = lax.broadcasted_iota(jnp.int32, (4 * ROWS, 128), 1)
    for rows, out in zip(refs[:count], refs[count + 3 : -1]):
        both = rows[...].reshape(4 * ROWS, D + 128)
        x = both[:, :D]
        w = jnp.where((lane == me) | (lane == me + 16), both[:, D:].astype(F32), 0.0)
        w = jnp.broadcast_to(jnp.sum(w, axis=1, keepdims=True), (4 * ROWS, 256))
        for n in range(FF // 256):
            c = slice(n * 256, (n + 1) * 256)
            g = jnp.dot(x, gate[0, :, c], preferred_element_type=F32)
            u = jnp.dot(x, up[0, :, c], preferred_element_type=F32)
            inner_s[:, c] = (g / (1.0 + jnp.exp(-g)) * u).astype(BF)
        inner = inner_s[...]
        for n in range(D // 256):
            c = slice(n * 256, (n + 1) * 256)
            res = jnp.dot(inner, down[0, :, c], preferred_element_type=F32).astype(BF).astype(F32)
            out[:, :, c] = (w * res).astype(BF).reshape(4, ROWS, 256)


def combine_kernel(keep, swap_in, s0, s1, s2, s3):
    for i, s in enumerate((s0, s1, s2, s3)):
        s[...] = (keep[i].astype(F32) + swap_in[i].astype(F32)).astype(s.dtype)


def total_kernel(s0, s1, s2, s3, out):
    out[...] = (s0[...] + s1[...].astype(F32) + s2[...].astype(F32) + s3[...].astype(F32)).astype(BF)


def final_kernel(hidden, s0, s1, s2, s3, far, out):
    mix = s0[...] + s1[...].astype(F32) + s2[...].astype(F32) + s3[...].astype(F32) + far[...].astype(F32)
    out[...] = (hidden[...].astype(F32) + mix).astype(BF)


def after(x, y):
    return lax.optimization_barrier((x, y))[0]


def swap_exp(x, mask):
    return lax.ppermute(x, "exp", [(i, i ^ mask) for i in range(16)])


def swap_ctx(x, mask):
    return lax.ppermute(x, "ctx", [(i, i ^ mask) for i in range(16)])


def turn_z(x, step):
    return lax.ppermute(x, "ctx", [(i, (i & 8) | ((i + step) & 7)) for i in range(16)])


def local(
    tokens,
    attn_gain,
    query_gain,
    key_gain,
    query_weight,
    key_weight,
    value_weight,
    out_weight,
    moe_gain,
    route_ids,
    route_weights,
    gate_weight,
    up_weight,
    down_weight,
):
    ctx = lax.axis_index("ctx").astype(jnp.int32)
    me = lax.axis_index("exp").astype(jnp.int32)
    y = (me >> 1) & 3
    info = jnp.stack([ctx, me, y, me >> 3, me & 1])
    planes = [list(range(8)), list(range(8, 16))]
    w_out = lax.all_gather(out_weight, "exp", axis=0, tiled=True, axis_index_groups=planes)

    [route] = call(route_kernel, (route_ids, route_weights), [((ROWS, 128), BF)], scalars=False)

    exponent = jnp.arange(HD // 2, dtype=F32) * (2.0 / HD)
    inverse = jnp.power(jnp.float32(ROPE_BASE), -exponent)
    owners = me ^ (2 * jnp.arange(4, dtype=jnp.int32))
    positions = (ctx * 1024 + owners[:, None] * ROWS + jnp.arange(ROWS, dtype=jnp.int32)[None, :]).reshape(-1)
    angles = positions.astype(F32)[:, None] * inverse[None, :]
    cosine, sine = jnp.cos(angles), jnp.sin(angles)
    cosine = jnp.concatenate([cosine, cosine], axis=1)
    sine = jnp.concatenate([-sine, sine], axis=1)

    w_far = swap_exp(query_weight, 8)
    w_core = swap_exp(query_weight, 1)
    [normed] = call(norm_kernel, (tokens, attn_gain[None]), [((ROWS, D), BF)], scalars=False, moved=MB)
    near = [swap_exp(normed, 2 * i) for i in (1, 2, 3)]
    own, other = call(
        kv_kernel,
        (info, normed, key_weight, value_weight, key_gain[None], cosine, sine),
        [((ROWS, 2 * HD), BF)] * 2,
        flops=ROWS * D * 1024,
        moved=2 * MB,
        in_hbm=(2, 3),
        scratch=[pltpu.VMEM((D, 2 * HD), BF), pltpu.VMEM((D, 2 * HD), BF), pltpu.SemaphoreType.DMA((2,))],
    )
    other = swap_exp(other, 8)
    w_far = after(w_far, (near, other))
    w_far_core = swap_exp(w_far, 1)
    pair = jnp.concatenate([own, other], axis=0)
    pair_in = swap_ctx(pair, 8)
    pair = jnp.stack([pair, pair_in])
    quad = jnp.stack([pair, turn_z(pair, 4)])
    below, above = turn_z(quad, 1), turn_z(quad, -1)
    keys = [quad, below, above, turn_z(below[:1], 1), turn_z(above[:1], -1)]

    mine, far = call(
        query_kernel,
        (info, normed, *near, query_weight, w_core, w_far, w_far_core, query_gain[None], cosine, sine),
        [((2, 256, HD), BF)] * 2,
        flops=256 * D * 1024,
        moved=4 * MB,
        scratch=[pltpu.VMEM((256, D), BF)],
    )
    far = swap_exp(after(far, pair_in), 8)
    both = jnp.stack([mine, after(far, quad)])
    parts = [swap_exp(both, 2 * i) for i in (1, 2, 3)]
    queries = jnp.stack([both] + after(parts, (below, above)))
    queries_core = swap_exp(queries, 1)
    def attend(which, q):
        return call(
            functools.partial(attend_kernel, which),
            (info, q, *keys),
            [((4, ROWS, WIDE), BF)],
            flops=2048 * 2048 * 512,
            moved=3 * MB,
            scratch=[
                pltpu.VMEM((2048, HD), BF),
                pltpu.VMEM((2048, 2 * HD), BF),
                pltpu.VMEM((512, 2 * HD), F32),
            ],
        )[0]

    def fold(part, part_core):
        parts = call(
            fold_kernel, (info, part, swap_exp(part_core, 1)), [((ROWS, WIDE), BF)] * 4, moved=2 * MB
        )
        return [parts[0]] + [swap_exp(parts[i], 2 * i) for i in (1, 2, 3)]

    a_far = attend(8, queries)
    a_far_core = attend(9, after(queries_core, a_far))
    a_near_core = attend(1, after(queries_core, (a_far_core, w_out)))
    a_near = attend(0, after(queries, a_near_core))
    sums_far, sums_near = fold(a_far, a_far_core), fold(a_near, a_near_core)
    part_in = swap_exp(project(after(sums_far, sums_near[0]), w_out, BF), 8)
    part = project(sums_near, w_out, F32)
    hidden, moe_in = call(
        hidden_kernel,
        (tokens, part, part_in, moe_gain[None], route),
        [((ROWS, D), BF), ((ROWS, D + 128), BF)],
        scalars=False,
        moved=2 * MB,
    )

    moe_far = swap_exp(moe_in, 8)
    near_1, near_2, near_3 = [swap_exp(moe_in, 2 * i) for i in (1, 2, 3)]
    m_near = jnp.stack(after([moe_in, near_1, near_2, near_3], moe_far))
    moe_far = after(moe_far, (near_1, near_3))
    far_1, far_3 = swap_exp(moe_far, 2), swap_exp(moe_far, 6)
    far_2 = swap_exp(after(moe_far, near_2), 4)

    def expert(*rows):
        return call(
            functools.partial(expert_kernel, len(rows)),
            (info, *rows, gate_weight, up_weight, down_weight),
            [((4, ROWS, D), BF)] * len(rows),
            flops=4 * ROWS * D * FF * 6 * len(rows),
            moved=12 * MB,
            limit=12,
            scratch=[pltpu.VMEM((4 * ROWS, FF), BF)],
        )

    def combine(keep, swap_in):
        s = call(
            combine_kernel,
            (keep, swap_in),
            [((ROWS, D), F32)] + [((ROWS, D), BF)] * 3,
            scalars=False,
            moved=4 * MB,
        )
        return [s[0]] + [swap_exp(s[i], 2 * i) for i in (1, 2, 3)]

    keep_near, swap_near = expert(m_near, swap_exp(m_near, 1))
    swap_near = swap_exp(after(swap_near, (far_1, far_3)), 1)
    m_far = jnp.stack(after([moe_far, far_1, far_2, far_3], keep_near))
    m_far_core = swap_exp(m_far, 1)
    [keep_far] = expert(m_far)
    [swap_far] = expert(after(m_far_core, keep_far))
    s_far = combine(keep_far, swap_exp(swap_far, 1))
    s_near = combine(keep_near, swap_near)
    [out_far] = call(total_kernel, tuple(s_far), [((ROWS, D), BF)], scalars=False, moved=2 * MB)
    [out] = call(
        final_kernel, (hidden, *s_near, swap_exp(out_far, 8)), [((ROWS, D), BF)], scalars=False, moved=2 * MB
    )
    return out


def solution(mesh):
    rows = P(("ctx", "exp"), None)
    return jax.shard_map(
        local,
        mesh=mesh,
        in_specs=(
            rows,
            P(),
            P(),
            P(),
            P(None, "exp"),
            P(),
            P(),
            P("exp", None),
            P(),
            rows,
            rows,
            P("exp", None, None),
            P("exp", None, None),
            P("exp", None, None),
        ),
        out_specs=rows,
        check_vma=False,
    )
```

```python
import functools

import jax
import jax.numpy as jnp
from jax import lax
from jax.experimental import pallas as pl
from jax.experimental.pallas import tpu as pltpu
from jax.sharding import PartitionSpec as P

EPS = 1e-06
ROPE_BASE = 1000000.0
HD = 128
D = 2048
FF = 768
ROWS = 64
WIDE = 8 * HD + 128
LOG2E = 1.4426950408889634
MB = 1 << 20
BF = jnp.bfloat16
F32 = jnp.float32

VM = pl.BlockSpec(memory_space=pltpu.VMEM)
SM = pl.BlockSpec(memory_space=pltpu.SMEM)
ANY = pl.BlockSpec(memory_space=pl.ANY)


def call(kernel, args, outs, flops=0, moved=0, scratch=(), scalars=True, limit=12, in_hbm=()):
    specs = [ANY if i in in_hbm else SM if scalars and i == 0 else VM for i in range(len(args))]
    return pl.pallas_call(
        kernel,
        out_shape=[jax.ShapeDtypeStruct(s, t) for s, t in outs],
        in_specs=specs,
        out_specs=[VM] * len(outs),
        scratch_shapes=list(scratch),
        compiler_params=pltpu.CompilerParams(vmem_limit_bytes=limit * MB),
        cost_estimate=pl.CostEstimate(flops=flops, bytes_accessed=moved, transcendentals=0),
    )(*args)


def rms(values, gain):
    factor = lax.rsqrt(jnp.mean(values * values, axis=-1, keepdims=True) + EPS)
    return values * factor * gain


def rope(values, cosine, sine):
    return values * cosine + pltpu.roll(values, HD // 2, 1) * sine


def norm_kernel(tokens, gain, out):
    out[...] = rms(tokens[...].astype(F32), gain[...]).astype(BF)


def kv_kernel(info, normed, key_weight, value_weight, gain, cosine, sine, own, other, kw, vw, sems):
    plane = info[3]
    loads = [pltpu.make_async_copy(key_weight, kw, sems.at[0]), pltpu.make_async_copy(value_weight, vw, sems.at[1])]
    for load in loads:
        load.start()
    x = normed[...]
    loads[0].wait()
    keys = jnp.dot(x, kw[...], preferred_element_type=F32)
    loads[1].wait()
    vals = jnp.dot(x, vw[...], preferred_element_type=F32).astype(BF)
    cos, sin = cosine[0:ROWS], sine[0:ROWS]
    k0 = rope(rms(keys[:, :HD], gain[...]), cos, sin)
    k1 = rope(rms(keys[:, HD:], gain[...]), cos, sin)
    v0, v1 = vals[:, :HD].astype(F32), vals[:, HD:].astype(F32)
    first = plane == 0
    own[:, :HD] = jnp.where(first, k0, k1).astype(BF)
    own[:, HD:] = jnp.where(first, v0, v1).astype(BF)
    other[:, :HD] = jnp.where(first, k1, k0).astype(BF)
    other[:, HD:] = jnp.where(first, v1, v0).astype(BF)


def query_kernel(info, r0, r1, r2, r3, w_own, w_core, w_far, w_far_core, gain, cosine, sine, mine, far, x_s):
    core = info[4]
    for i, r in enumerate((r0, r1, r2, r3)):
        x_s[i * ROWS : (i + 1) * ROWS] = r[...]
    x = x_s[...]
    cos, sin = cosine[...], sine[...]
    scale = gain[...] * (LOG2E * HD**-0.5)
    for out, first, second in ((far, w_far, w_far_core), (mine, w_own, w_core)):
        q = jnp.dot(x, jnp.concatenate([first[...], second[...]], axis=1), preferred_element_type=F32)
        out[core] = rope(rms(q[:, :HD], scale), cos, sin).astype(BF)
        out[1 - core] = rope(rms(q[:, HD:], scale), cos, sin).astype(BF)


KEYS = 512


def attend_kernel(which, info, q, t0, t1, t2, t3, t4, out, k_s, v_s, acc):
    ctx, me = info[0], info[1]
    base = jnp.bitwise_xor(me, which)
    y = jnp.bitwise_and(jnp.right_shift(me, 1), 3)
    at = 0
    for t, distance in ((t0, (0, 4)), (t1, (-1, 3)), (t2, (1, 5)), (t3, (-2,)), (t4, (2,))):
        for j, d in enumerate(distance):
            for i in range(2):
                z = jnp.bitwise_and(ctx + (8 + d), 7)
                source = jnp.bitwise_and(jnp.bitwise_xor(ctx, 8 * i), 8) + z
                valid = source <= ctx
                k_s[at : at + 128] = t[j, i, :, :HD]
                v_s[at : at + 128, :HD] = jnp.where(valid, t[j, i, :, HD:].astype(F32), 0.0).astype(BF)
                v_s[at : at + 128, HD:] = jnp.full((128, HD), jnp.where(valid, 1.0, 0.0), F32).astype(BF)
                at += 128
    out[:, :, 8 * HD :] = jnp.zeros((4, ROWS, 128), BF)
    lane = lax.broadcasted_iota(jnp.int32, (ROWS, 128), 1)

    def per_piece(dd, carry):
        row = lax.broadcasted_iota(jnp.int32, (256, 1), 0)
        key = lax.broadcasted_iota(jnp.int32, (256, 128), 1)
        key_dev = jnp.bitwise_xor(me, jnp.bitwise_and(jnp.right_shift(key, 6), 1) * 8)
        row_dev = jnp.bitwise_xor(base, jnp.bitwise_xor(jnp.right_shift(row, 6), dd) * 2)
        allowed = key_dev * ROWS + jnp.bitwise_and(key, 63) <= row_dev * ROWS + jnp.bitwise_and(row, 63)
        for p in range(2):
            qv = q[dd, which >> 3, p]
            total = None
            for c in range(0, 2048, KEYS):
                s = lax.dot_general(
                    qv, k_s[c : c + KEYS], (((1,), (1,)), ((), ())), preferred_element_type=F32
                )
                w = jnp.exp2(s)
                if c == 0:
                    w = jnp.concatenate([jnp.where(allowed, w[:, :128], 0.0), w[:, 128:]], axis=1)
                o = jnp.dot(w.astype(BF), v_s[c : c + KEYS], preferred_element_type=F32)
                total = o if total is None else total + o
            acc[p * 256 : (p + 1) * 256] = total
        for p in range(2):
            head = jnp.bitwise_xor(y, dd) * 2 + p
            for i in range(4):
                rows = jnp.bitwise_xor(jnp.bitwise_xor(y, dd), i)
                block = acc[p * 256 + i * ROWS : p * 256 + (i + 1) * ROWS]
                out[rows, :, pl.ds(pl.multiple_of(head * HD, HD), HD)] = block[:, :HD].astype(BF)
                den = block[:, HD:]
                high = den.astype(BF).astype(F32)
                old = out[rows, :, 8 * HD :].astype(F32)
                new = jnp.where(lane == head, high, jnp.where(lane == head + 8, den - high, old))
                out[rows, :, 8 * HD :] = new.astype(BF)
        return carry

    lax.fori_loop(0, 4, per_piece, 0, unroll=True)


def fold_kernel(info, part, part_in, s0, s1, s2, s3):
    y = info[2]
    for i, s in enumerate((s0, s1, s2, s3)):
        at = jnp.bitwise_xor(y, i)
        s[...] = (part[at].astype(F32) + part_in[at].astype(F32)).astype(BF)


def attended(s0, s1, s2, s3, x_s):
    total = s0[...].astype(F32) + s1[...].astype(F32) + s2[...].astype(F32) + s3[...].astype(F32)
    for h in range(8):
        den = total[:, 8 * HD + h : 8 * HD + h + 1] + total[:, 8 * HD + 8 + h : 8 * HD + 9 + h]
        x_s[:, h * HD : (h + 1) * HD] = (total[:, h * HD : (h + 1) * HD] / den).astype(BF)
    return x_s[...]


def project_kernel(s0, s1, s2, s3, weight, out, x_s):
    x = attended(s0, s1, s2, s3, x_s)
    for n in range(4):
        c = slice(n * 512, (n + 1) * 512)
        out[:, c] = jnp.dot(x, weight[:, c], preferred_element_type=F32).astype(BF)


def hidden_kernel(s0, s1, s2, s3, weight, tokens, part_in, gain, route, hidden, moe_in, x_s):
    x = attended(s0, s1, s2, s3, x_s)
    for n in range(4):
        c = slice(n * 512, (n + 1) * 512)
        part = jnp.dot(x, weight[:, c], preferred_element_type=F32)
        hidden[:, c] = (tokens[:, c].astype(F32) + (part + part_in[:, c].astype(F32))).astype(BF)
    moe_in[:, :D] = rms(hidden[...].astype(F32), gain[...]).astype(BF)
    moe_in[:, D:] = route[...]


def route_kernel(ids, weights, out):
    lane = lax.broadcasted_iota(jnp.int32, (ROWS, 128), 1)
    table = jnp.zeros((ROWS, 128), F32)
    for k in range(8):
        expert, weight = ids[:, k : k + 1], weights[:, k : k + 1]
        high = weight.astype(BF).astype(F32)
        table = jnp.where(lane == expert, high, jnp.where(lane == expert + 16, weight - high, table))
    out[...] = table.astype(BF)


def expert_kernel(count, info, *refs):
    me = info[1]
    gate, up, down = refs[count : count + 3]
    inner_s = refs[-1]
    lane = lax.broadcasted_iota(jnp.int32, (4 * ROWS, 128), 1)
    for rows, out in zip(refs[:count], refs[count + 3 : -1]):
        both = rows[...].reshape(4 * ROWS, D + 128)
        x = both[:, :D]
        w = jnp.where((lane == me) | (lane == me + 16), both[:, D:].astype(F32), 0.0)
        w = jnp.broadcast_to(jnp.sum(w, axis=1, keepdims=True), (4 * ROWS, 256))
        for n in range(FF // 256):
            c = slice(n * 256, (n + 1) * 256)
            g = jnp.dot(x, gate[0, :, c], preferred_element_type=F32)
            u = jnp.dot(x, up[0, :, c], preferred_element_type=F32)
            inner_s[:, c] = (g / (1.0 + jnp.exp(-g)) * u).astype(BF)
        inner = inner_s[...]
        for n in range(D // 256):
            c = slice(n * 256, (n + 1) * 256)
            res = jnp.dot(inner, down[0, :, c], preferred_element_type=F32).astype(BF).astype(F32)
            out[:, :, c] = (w * res).astype(BF).reshape(4, ROWS, 256)


def combine_kernel(keep, swap_in, s0, s1, s2, s3):
    for i, s in enumerate((s0, s1, s2, s3)):
        s[...] = (keep[i].astype(F32) + swap_in[i].astype(F32)).astype(s.dtype)


def total_kernel(s0, s1, s2, s3, out):
    out[...] = (s0[...] + s1[...].astype(F32) + s2[...].astype(F32) + s3[...].astype(F32)).astype(BF)


def final_kernel(hidden, s0, s1, s2, s3, far, out):
    mix = s0[...] + s1[...].astype(F32) + s2[...].astype(F32) + s3[...].astype(F32) + far[...].astype(F32)
    out[...] = (hidden[...].astype(F32) + mix).astype(BF)


def after(x, y):
    return lax.optimization_barrier((x, y))[0]


def swap_exp(x, mask):
    return lax.ppermute(x, "exp", [(i, i ^ mask) for i in range(16)])


def swap_ctx(x, mask):
    return lax.ppermute(x, "ctx", [(i, i ^ mask) for i in range(16)])


def turn_z(x, step):
    return lax.ppermute(x, "ctx", [(i, (i & 8) | ((i + step) & 7)) for i in range(16)])


def local(
    tokens,
    attn_gain,
    query_gain,
    key_gain,
    query_weight,
    key_weight,
    value_weight,
    out_weight,
    moe_gain,
    route_ids,
    route_weights,
    gate_weight,
    up_weight,
    down_weight,
):
    ctx = lax.axis_index("ctx").astype(jnp.int32)
    me = lax.axis_index("exp").astype(jnp.int32)
    y = (me >> 1) & 3
    info = jnp.stack([ctx, me, y, me >> 3, me & 1])
    planes = [list(range(8)), list(range(8, 16))]
    w_out = lax.all_gather(out_weight, "exp", axis=0, tiled=True, axis_index_groups=planes)

    [route] = call(route_kernel, (route_ids, route_weights), [((ROWS, 128), BF)], scalars=False)

    exponent = jnp.arange(HD // 2, dtype=F32) * (2.0 / HD)
    inverse = jnp.power(jnp.float32(ROPE_BASE), -exponent)
    owners = me ^ (2 * jnp.arange(4, dtype=jnp.int32))
    positions = (ctx * 1024 + owners[:, None] * ROWS + jnp.arange(ROWS, dtype=jnp.int32)[None, :]).reshape(-1)
    angles = positions.astype(F32)[:, None] * inverse[None, :]
    cosine, sine = jnp.cos(angles), jnp.sin(angles)
    cosine = jnp.concatenate([cosine, cosine], axis=1)
    sine = jnp.concatenate([-sine, sine], axis=1)

    w_far = swap_exp(query_weight, 8)
    w_core = swap_exp(query_weight, 1)
    [normed] = call(norm_kernel, (tokens, attn_gain[None]), [((ROWS, D), BF)], scalars=False, moved=MB)
    near = [swap_exp(normed, 2 * i) for i in (1, 2, 3)]
    own, other = call(
        kv_kernel,
        (info, normed, key_weight, value_weight, key_gain[None], cosine, sine),
        [((ROWS, 2 * HD), BF)] * 2,
        flops=ROWS * D * 1024,
        moved=2 * MB,
        in_hbm=(2, 3),
        scratch=[pltpu.VMEM((D, 2 * HD), BF), pltpu.VMEM((D, 2 * HD), BF), pltpu.SemaphoreType.DMA((2,))],
    )
    other = swap_exp(other, 8)
    w_far = after(w_far, (near, other))
    w_far_core = swap_exp(w_far, 1)
    pair = jnp.concatenate([own, other], axis=0)
    pair_in = swap_ctx(pair, 8)
    pair = jnp.stack([pair, pair_in])
    quad = jnp.stack([pair, turn_z(pair, 4)])
    below, above = turn_z(quad, 1), turn_z(quad, -1)
    keys = [quad, below, above, turn_z(below[:1], 1), turn_z(above[:1], -1)]

    mine, far = call(
        query_kernel,
        (info, normed, *near, query_weight, w_core, w_far, w_far_core, query_gain[None], cosine, sine),
        [((2, 256, HD), BF)] * 2,
        flops=256 * D * 1024,
        moved=4 * MB,
        scratch=[pltpu.VMEM((256, D), BF)],
    )
    far = swap_exp(after(far, pair_in), 8)
    both = jnp.stack([mine, after(far, quad)])
    parts = [swap_exp(both, 2 * i) for i in (1, 2, 3)]
    queries = jnp.stack([both] + after(parts, keys[1:]))
    queries_core = swap_exp(queries, 1)
    def attend(which, q):
        return call(
            functools.partial(attend_kernel, which),
            (info, q, *keys),
            [((4, ROWS, WIDE), BF)],
            flops=2048 * 2048 * 512,
            moved=3 * MB,
            scratch=[
                pltpu.VMEM((2048, HD), BF),
                pltpu.VMEM((2048, 2 * HD), BF),
                pltpu.VMEM((512, 2 * HD), F32),
            ],
        )[0]

    def fold(part, part_core):
        parts = call(
            fold_kernel, (info, part, swap_exp(part_core, 1)), [((ROWS, WIDE), BF)] * 4, moved=2 * MB
        )
        return [parts[0]] + [swap_exp(parts[i], 2 * i) for i in (1, 2, 3)]

    a_far = attend(8, queries)
    a_far_core = attend(9, after(queries_core, a_far))
    a_near_core = attend(1, after(queries_core, (a_far_core, w_out)))
    a_near = attend(0, after(queries, a_near_core))
    sums_far, sums_near = fold(a_far, a_far_core), fold(a_near, a_near_core)
    [part_far] = call(
        project_kernel,
        (*after(sums_far, sums_near[0]), w_out),
        [((ROWS, D), BF)],
        scalars=False,
        flops=ROWS * 2048 * 2048,
        moved=5 * MB,
        scratch=[pltpu.VMEM((ROWS, 8 * HD), BF)],
    )
    hidden, moe_in = call(
        hidden_kernel,
        (*sums_near, w_out, tokens, swap_exp(part_far, 8), moe_gain[None], route),
        [((ROWS, D), BF), ((ROWS, D + 128), BF)],
        scalars=False,
        flops=ROWS * 2048 * 2048,
        moved=5 * MB,
        scratch=[pltpu.VMEM((ROWS, 8 * HD), BF)],
    )

    moe_far = swap_exp(moe_in, 8)
    near_1, near_2, near_3 = [swap_exp(moe_in, 2 * i) for i in (1, 2, 3)]
    m_near = jnp.stack(after([moe_in, near_1, near_2, near_3], moe_far))
    moe_far = after(moe_far, (near_1, near_3))
    far_1, far_3 = swap_exp(moe_far, 2), swap_exp(moe_far, 6)
    far_2 = swap_exp(after(moe_far, near_2), 4)

    def expert(*rows):
        return call(
            functools.partial(expert_kernel, len(rows)),
            (info, *rows, gate_weight, up_weight, down_weight),
            [((4, ROWS, D), BF)] * len(rows),
            flops=4 * ROWS * D * FF * 6 * len(rows),
            moved=12 * MB,
            limit=12,
            scratch=[pltpu.VMEM((4 * ROWS, FF), BF)],
        )

    def combine(keep, swap_in):
        s = call(
            combine_kernel,
            (keep, swap_in),
            [((ROWS, D), F32)] + [((ROWS, D), BF)] * 3,
            scalars=False,
            moved=4 * MB,
        )
        return [s[0]] + [swap_exp(s[i], 2 * i) for i in (1, 2, 3)]

    keep_near, swap_near = expert(m_near, swap_exp(m_near, 1))
    swap_near = swap_exp(after(swap_near, (far_1, far_3)), 1)
    m_far = jnp.stack(after([moe_far, far_1, far_2, far_3], keep_near))
    m_far_core = swap_exp(m_far, 1)
    [keep_far] = expert(m_far)
    [swap_far] = expert(after(m_far_core, keep_far))
    s_far = combine(keep_far, swap_exp(swap_far, 1))
    s_near = combine(keep_near, swap_near)
    [out_far] = call(total_kernel, tuple(s_far), [((ROWS, D), BF)], scalars=False, moved=2 * MB)
    [out] = call(
        final_kernel, (hidden, *s_near, swap_exp(out_far, 8)), [((ROWS, D), BF)], scalars=False, moved=2 * MB
    )
    return out


def solution(mesh):
    rows = P(("ctx", "exp"), None)
    return jax.shard_map(
        local,
        mesh=mesh,
        in_specs=(
            rows,
            P(),
            P(),
            P(),
            P(None, "exp"),
            P(),
            P(),
            P("exp", None),
            P(),
            rows,
            rows,
            P("exp", None, None),
            P("exp", None, None),
            P("exp", None, None),
        ),
        out_specs=rows,
        check_vma=False,
    )
```

```python
import functools

import jax
import jax.numpy as jnp
from jax import lax
from jax.experimental import pallas as pl
from jax.experimental.pallas import tpu as pltpu
from jax.sharding import PartitionSpec as P

EPS = 1e-06
ROPE_BASE = 1000000.0
HD = 128
D = 2048
FF = 768
ROWS = 64
WIDE = 8 * HD + 128
LOG2E = 1.4426950408889634
MB = 1 << 20
BF = jnp.bfloat16
F32 = jnp.float32

VM = pl.BlockSpec(memory_space=pltpu.VMEM)
SM = pl.BlockSpec(memory_space=pltpu.SMEM)
ANY = pl.BlockSpec(memory_space=pl.ANY)


def call(kernel, args, outs, flops=0, moved=0, scratch=(), scalars=True, limit=12, in_hbm=()):
    specs = [ANY if i in in_hbm else SM if scalars and i == 0 else VM for i in range(len(args))]
    return pl.pallas_call(
        kernel,
        out_shape=[jax.ShapeDtypeStruct(s, t) for s, t in outs],
        in_specs=specs,
        out_specs=[VM] * len(outs),
        scratch_shapes=list(scratch),
        compiler_params=pltpu.CompilerParams(vmem_limit_bytes=limit * MB),
        cost_estimate=pl.CostEstimate(flops=flops, bytes_accessed=moved, transcendentals=0),
    )(*args)


def rms(values, gain):
    factor = lax.rsqrt(jnp.mean(values * values, axis=-1, keepdims=True) + EPS)
    return values * factor * gain


def rope(values, cosine, sine):
    return values * cosine + pltpu.roll(values, HD // 2, 1) * sine


def norm_kernel(tokens, gain, out):
    out[...] = rms(tokens[...].astype(F32), gain[...]).astype(BF)


def kv_kernel(info, normed, key_weight, value_weight, gain, cosine, sine, own, other, kw, vw, sems):
    plane = info[3]
    loads = [pltpu.make_async_copy(key_weight, kw, sems.at[0]), pltpu.make_async_copy(value_weight, vw, sems.at[1])]
    for load in loads:
        load.start()
    x = normed[...]
    loads[0].wait()
    keys = jnp.dot(x, kw[...], preferred_element_type=F32)
    loads[1].wait()
    vals = jnp.dot(x, vw[...], preferred_element_type=F32).astype(BF)
    cos, sin = cosine[0:ROWS], sine[0:ROWS]
    k0 = rope(rms(keys[:, :HD], gain[...]), cos, sin)
    k1 = rope(rms(keys[:, HD:], gain[...]), cos, sin)
    v0, v1 = vals[:, :HD].astype(F32), vals[:, HD:].astype(F32)
    first = plane == 0
    own[:, :HD] = jnp.where(first, k0, k1).astype(BF)
    own[:, HD:] = jnp.where(first, v0, v1).astype(BF)
    other[:, :HD] = jnp.where(first, k1, k0).astype(BF)
    other[:, HD:] = jnp.where(first, v1, v0).astype(BF)


def query_kernel(info, r0, r1, r2, r3, w_own, w_core, w_far, w_far_core, gain, cosine, sine, mine, far, x_s):
    core = info[4]
    for i, r in enumerate((r0, r1, r2, r3)):
        x_s[i * ROWS : (i + 1) * ROWS] = r[...]
    x = x_s[...]
    cos, sin = cosine[...], sine[...]
    scale = gain[...] * (LOG2E * HD**-0.5)
    for out, first, second in ((far, w_far, w_far_core), (mine, w_own, w_core)):
        q = jnp.dot(x, jnp.concatenate([first[...], second[...]], axis=1), preferred_element_type=F32)
        out[core] = rope(rms(q[:, :HD], scale), cos, sin).astype(BF)
        out[1 - core] = rope(rms(q[:, HD:], scale), cos, sin).astype(BF)


KEYS = 512


def attend_kernel(which, info, q, t0, t1, t2, t3, t4, out, k_s, v_s, acc):
    ctx, me = info[0], info[1]
    base = jnp.bitwise_xor(me, which)
    y = jnp.bitwise_and(jnp.right_shift(me, 1), 3)
    at = 0
    for t, distance in ((t0, (0, 4)), (t1, (-1, 3)), (t2, (1, 5)), (t3, (-2,)), (t4, (2,))):
        for j, d in enumerate(distance):
            for i in range(2):
                z = jnp.bitwise_and(ctx + (8 + d), 7)
                source = jnp.bitwise_and(jnp.bitwise_xor(ctx, 8 * i), 8) + z
                valid = source <= ctx
                k_s[at : at + 128] = t[j, i, :, :HD]
                v_s[at : at + 128, :HD] = jnp.where(valid, t[j, i, :, HD:].astype(F32), 0.0).astype(BF)
                v_s[at : at + 128, HD:] = jnp.full((128, HD), jnp.where(valid, 1.0, 0.0), F32).astype(BF)
                at += 128
    out[:, :, 8 * HD :] = jnp.zeros((4, ROWS, 128), BF)
    lane = lax.broadcasted_iota(jnp.int32, (ROWS, 128), 1)

    def per_piece(dd, carry):
        row = lax.broadcasted_iota(jnp.int32, (256, 1), 0)
        key = lax.broadcasted_iota(jnp.int32, (256, 128), 1)
        key_dev = jnp.bitwise_xor(me, jnp.bitwise_and(jnp.right_shift(key, 6), 1) * 8)
        row_dev = jnp.bitwise_xor(base, jnp.bitwise_xor(jnp.right_shift(row, 6), dd) * 2)
        allowed = key_dev * ROWS + jnp.bitwise_and(key, 63) <= row_dev * ROWS + jnp.bitwise_and(row, 63)
        for p in range(2):
            qv = q[dd, which >> 3, p]
            total = None
            for c in range(0, 2048, KEYS):
                s = lax.dot_general(
                    qv, k_s[c : c + KEYS], (((1,), (1,)), ((), ())), preferred_element_type=F32
                )
                w = jnp.exp2(s)
                if c == 0:
                    w = jnp.concatenate([jnp.where(allowed, w[:, :128], 0.0), w[:, 128:]], axis=1)
                o = jnp.dot(w.astype(BF), v_s[c : c + KEYS], preferred_element_type=F32)
                total = o if total is None else total + o
            acc[p * 256 : (p + 1) * 256] = total
        for p in range(2):
            head = jnp.bitwise_xor(y, dd) * 2 + p
            for i in range(4):
                rows = jnp.bitwise_xor(jnp.bitwise_xor(y, dd), i)
                block = acc[p * 256 + i * ROWS : p * 256 + (i + 1) * ROWS]
                out[rows, :, pl.ds(pl.multiple_of(head * HD, HD), HD)] = block[:, :HD].astype(BF)
                den = block[:, HD:]
                high = den.astype(BF).astype(F32)
                old = out[rows, :, 8 * HD :].astype(F32)
                new = jnp.where(lane == head, high, jnp.where(lane == head + 8, den - high, old))
                out[rows, :, 8 * HD :] = new.astype(BF)
        return carry

    lax.fori_loop(0, 4, per_piece, 0, unroll=True)


def fold_kernel(info, part, part_in, s0, s1, s2, s3):
    y = info[2]
    for i, s in enumerate((s0, s1, s2, s3)):
        at = jnp.bitwise_xor(y, i)
        s[...] = (part[at].astype(F32) + part_in[at].astype(F32)).astype(BF)


def attended(s0, s1, s2, s3, x_s):
    total = s0[...].astype(F32) + s1[...].astype(F32) + s2[...].astype(F32) + s3[...].astype(F32)
    for h in range(8):
        den = total[:, 8 * HD + h : 8 * HD + h + 1] + total[:, 8 * HD + 8 + h : 8 * HD + 9 + h]
        x_s[:, h * HD : (h + 1) * HD] = (total[:, h * HD : (h + 1) * HD] / den).astype(BF)
    return x_s[...]


def project_kernel(s0, s1, s2, s3, weight, out, x_s):
    x = attended(s0, s1, s2, s3, x_s)
    for n in range(4):
        c = slice(n * 512, (n + 1) * 512)
        out[:, c] = jnp.dot(x, weight[:, c], preferred_element_type=F32).astype(BF)


def hidden_kernel(s0, s1, s2, s3, weight, tokens, part_in, gain, route, hidden, moe_in, x_s):
    x = attended(s0, s1, s2, s3, x_s)
    for n in range(4):
        c = slice(n * 512, (n + 1) * 512)
        part = jnp.dot(x, weight[:, c], preferred_element_type=F32)
        hidden[:, c] = (tokens[:, c].astype(F32) + (part + part_in[:, c].astype(F32))).astype(BF)
    moe_in[:, :D] = rms(hidden[...].astype(F32), gain[...]).astype(BF)
    moe_in[:, D:] = route[...]


def route_kernel(ids, weights, out):
    lane = lax.broadcasted_iota(jnp.int32, (ROWS, 128), 1)
    table = jnp.zeros((ROWS, 128), F32)
    for k in range(8):
        expert, weight = ids[:, k : k + 1], weights[:, k : k + 1]
        high = weight.astype(BF).astype(F32)
        table = jnp.where(lane == expert, high, jnp.where(lane == expert + 16, weight - high, table))
    out[...] = table.astype(BF)


def expert_kernel(count, info, *refs):
    me = info[1]
    gate, up, down = refs[count : count + 3]
    inner_s = refs[-1]
    lane = lax.broadcasted_iota(jnp.int32, (4 * ROWS, 128), 1)
    for rows, out in zip(refs[:count], refs[count + 3 : -1]):
        both = rows[...].reshape(4 * ROWS, D + 128)
        x = both[:, :D]
        w = jnp.where((lane == me) | (lane == me + 16), both[:, D:].astype(F32), 0.0)
        w = jnp.broadcast_to(jnp.sum(w, axis=1, keepdims=True), (4 * ROWS, 256))
        for n in range(FF // 256):
            c = slice(n * 256, (n + 1) * 256)
            g = jnp.dot(x, gate[0, :, c], preferred_element_type=F32)
            u = jnp.dot(x, up[0, :, c], preferred_element_type=F32)
            inner_s[:, c] = (g / (1.0 + jnp.exp(-g)) * u).astype(BF)
        inner = inner_s[...]
        for n in range(D // 256):
            c = slice(n * 256, (n + 1) * 256)
            res = jnp.dot(inner, down[0, :, c], preferred_element_type=F32).astype(BF).astype(F32)
            out[:, :, c] = (w * res).astype(BF).reshape(4, ROWS, 256)


def combine_kernel(keep, swap_in, s0, s1, s2, s3):
    for i, s in enumerate((s0, s1, s2, s3)):
        s[...] = (keep[i].astype(F32) + swap_in[i].astype(F32)).astype(s.dtype)


def total_kernel(s0, s1, s2, s3, out):
    out[...] = (s0[...] + s1[...].astype(F32) + s2[...].astype(F32) + s3[...].astype(F32)).astype(BF)


def final_kernel(hidden, s0, s1, s2, s3, far, out):
    mix = s0[...] + s1[...].astype(F32) + s2[...].astype(F32) + s3[...].astype(F32) + far[...].astype(F32)
    out[...] = (hidden[...].astype(F32) + mix).astype(BF)


def after(x, y):
    return lax.optimization_barrier((x, y))[0]


def swap_exp(x, mask):
    return lax.ppermute(x, "exp", [(i, i ^ mask) for i in range(16)])


def swap_ctx(x, mask):
    return lax.ppermute(x, "ctx", [(i, i ^ mask) for i in range(16)])


def turn_z(x, step):
    return lax.ppermute(x, "ctx", [(i, (i & 8) | ((i + step) & 7)) for i in range(16)])


def local(
    tokens,
    attn_gain,
    query_gain,
    key_gain,
    query_weight,
    key_weight,
    value_weight,
    out_weight,
    moe_gain,
    route_ids,
    route_weights,
    gate_weight,
    up_weight,
    down_weight,
):
    ctx = lax.axis_index("ctx").astype(jnp.int32)
    me = lax.axis_index("exp").astype(jnp.int32)
    y = (me >> 1) & 3
    info = jnp.stack([ctx, me, y, me >> 3, me & 1])
    planes = [list(range(8)), list(range(8, 16))]
    w_out = lax.all_gather(out_weight, "exp", axis=0, tiled=True, axis_index_groups=planes)

    [route] = call(route_kernel, (route_ids, route_weights), [((ROWS, 128), BF)], scalars=False)

    exponent = jnp.arange(HD // 2, dtype=F32) * (2.0 / HD)
    inverse = jnp.power(jnp.float32(ROPE_BASE), -exponent)
    owners = me ^ (2 * jnp.arange(4, dtype=jnp.int32))
    positions = (ctx * 1024 + owners[:, None] * ROWS + jnp.arange(ROWS, dtype=jnp.int32)[None, :]).reshape(-1)
    angles = positions.astype(F32)[:, None] * inverse[None, :]
    cosine, sine = jnp.cos(angles), jnp.sin(angles)
    cosine = jnp.concatenate([cosine, cosine], axis=1)
    sine = jnp.concatenate([-sine, sine], axis=1)

    w_far = swap_exp(query_weight, 8)
    w_core = swap_exp(query_weight, 1)
    [normed] = call(norm_kernel, (tokens, attn_gain[None]), [((ROWS, D), BF)], scalars=False, moved=MB)
    near = [swap_exp(normed, 2 * i) for i in (1, 2, 3)]
    own, other = call(
        kv_kernel,
        (info, normed, key_weight, value_weight, key_gain[None], cosine, sine),
        [((ROWS, 2 * HD), BF)] * 2,
        flops=ROWS * D * 1024,
        moved=2 * MB,
        in_hbm=(2, 3),
        scratch=[pltpu.VMEM((D, 2 * HD), BF), pltpu.VMEM((D, 2 * HD), BF), pltpu.SemaphoreType.DMA((2,))],
    )
    other = swap_exp(other, 8)
    w_far = after(w_far, (near, other))
    w_far_core = swap_exp(w_far, 1)
    pair = jnp.concatenate([own, other], axis=0)
    pair_in = swap_ctx(pair, 8)
    pair = jnp.stack([pair, pair_in])
    quad = jnp.stack([pair, turn_z(pair, 4)])
    below, above = turn_z(quad, 1), turn_z(quad, -1)
    keys = [quad, below, above, turn_z(below[:1], 1), turn_z(above[:1], -1)]

    mine, far = call(
        query_kernel,
        (info, normed, *near, query_weight, w_core, w_far, w_far_core, query_gain[None], cosine, sine),
        [((2, 256, HD), BF)] * 2,
        flops=256 * D * 1024,
        moved=4 * MB,
        scratch=[pltpu.VMEM((256, D), BF)],
    )
    far = swap_exp(after(far, pair_in), 8)
    both = jnp.stack([mine, after(far, quad)])
    parts = [swap_exp(both, 2 * i) for i in (1, 2, 3)]
    queries = jnp.stack([both] + after(parts, keys[1:]))
    queries_core = swap_exp(queries, 1)
    def attend(which, q):
        return call(
            functools.partial(attend_kernel, which),
            (info, q, *keys),
            [((4, ROWS, WIDE), BF)],
            flops=2048 * 2048 * 512,
            moved=3 * MB,
            scratch=[
                pltpu.VMEM((2048, HD), BF),
                pltpu.VMEM((2048, 2 * HD), BF),
                pltpu.VMEM((512, 2 * HD), F32),
            ],
        )[0]

    def fold(part, part_core):
        parts = call(
            fold_kernel, (info, part, swap_exp(part_core, 1)), [((ROWS, WIDE), BF)] * 4, moved=2 * MB
        )
        return [parts[0]] + [swap_exp(parts[i], 2 * i) for i in (1, 2, 3)]

    a_far = attend(8, after(queries, w_out))
    a_far_core = attend(9, after(queries_core, a_far))
    a_near_core = attend(1, after(queries_core, a_far_core))
    a_near = attend(0, after(queries, a_near_core))
    sums_far, sums_near = fold(a_far, a_far_core), fold(a_near, a_near_core)
    [part_far] = call(
        project_kernel,
        (*after(sums_far, sums_near[0]), w_out),
        [((ROWS, D), BF)],
        scalars=False,
        flops=ROWS * 2048 * 2048,
        moved=5 * MB,
        scratch=[pltpu.VMEM((ROWS, 8 * HD), BF)],
    )
    hidden, moe_in = call(
        hidden_kernel,
        (*sums_near, w_out, tokens, swap_exp(part_far, 8), moe_gain[None], route),
        [((ROWS, D), BF), ((ROWS, D + 128), BF)],
        scalars=False,
        flops=ROWS * 2048 * 2048,
        moved=5 * MB,
        scratch=[pltpu.VMEM((ROWS, 8 * HD), BF)],
    )

    moe_far = swap_exp(moe_in, 8)
    near_1, near_2, near_3 = [swap_exp(moe_in, 2 * i) for i in (1, 2, 3)]
    m_near = jnp.stack(after([moe_in, near_1, near_2, near_3], moe_far))
    moe_far = after(moe_far, (near_1, near_3))
    far_1, far_3 = swap_exp(moe_far, 2), swap_exp(moe_far, 6)
    far_2 = swap_exp(after(moe_far, near_2), 4)

    def expert(*rows):
        return call(
            functools.partial(expert_kernel, len(rows)),
            (info, *rows, gate_weight, up_weight, down_weight),
            [((4, ROWS, D), BF)] * len(rows),
            flops=4 * ROWS * D * FF * 6 * len(rows),
            moved=12 * MB,
            limit=12,
            scratch=[pltpu.VMEM((4 * ROWS, FF), BF)],
        )

    def combine(keep, swap_in):
        s = call(
            combine_kernel,
            (keep, swap_in),
            [((ROWS, D), F32)] + [((ROWS, D), BF)] * 3,
            scalars=False,
            moved=4 * MB,
        )
        return [s[0]] + [swap_exp(s[i], 2 * i) for i in (1, 2, 3)]

    keep_near, swap_near = expert(m_near, swap_exp(m_near, 1))
    swap_near = swap_exp(after(swap_near, (far_1, far_3)), 1)
    m_far = jnp.stack(after([moe_far, far_1, far_2, far_3], keep_near))
    m_far_core = swap_exp(m_far, 1)
    [keep_far] = expert(m_far)
    [swap_far] = expert(after(m_far_core, keep_far))
    s_far = combine(keep_far, swap_exp(swap_far, 1))
    s_near = combine(keep_near, swap_near)
    [out_far] = call(total_kernel, tuple(s_far), [((ROWS, D), BF)], scalars=False, moved=2 * MB)
    [out] = call(
        final_kernel, (hidden, *s_near, swap_exp(out_far, 8)), [((ROWS, D), BF)], scalars=False, moved=2 * MB
    )
    return out


def solution(mesh):
    rows = P(("ctx", "exp"), None)
    return jax.shard_map(
        local,
        mesh=mesh,
        in_specs=(
            rows,
            P(),
            P(),
            P(),
            P(None, "exp"),
            P(),
            P(),
            P("exp", None),
            P(),
            rows,
            rows,
            P("exp", None, None),
            P("exp", None, None),
            P("exp", None, None),
        ),
        out_specs=rows,
        check_vma=False,
    )
```
